512 devices in a mesh: section: 64 (over y, z_lo, core), dp: 8 (over x, z_hi).
Axes of the slice: x: 4, y: 8, z: 8 (z_hi: 2, z_lo: 4; z = z_hi * 4 + z_lo), core: 2. Of those that a mesh axis runs over, the one named last changes fastest.
Arguments:
- inputs: bfloat16 [8, 128, 8192], P(None, 'dp', 'section'), may hold values from -6 to 6
- gain: float32 [64, 8192], P('section'), may hold values from 0.1 to 1.9
- w_in: bfloat16 [64, 8192, 128], P('section'), may hold values from -0.0625 to 0.0625
- w_out: bfloat16 [64, 128, 8192], P('section'), may hold values from -0.5 to 0.5
Outputs:
- grad_in: bfloat16 [64, 8192, 128], P('section', 'dp')
- grad_out: bfloat16 [64, 128, 8192], P('section', None, 'dp')
The draws below stay inside these ranges and needn't reach their ends.
All inputs are finite; a program needn't handle non-finite values.
Results may differ from the reference program's by a relative error of at most 0.034.
Values may be sent and summed in bfloat16 or wider, within the bound.
No kernel may reach another device: no remote copies, remote signals or barrier semaphores. Data moves between devices by JAX's collectives and lax.ppermute only.
A program may use at most 64 MiB of HBM per device.

```python
import math
import jax
import jax.numpy as jnp
from jax import lax

D = 8192
HD = 128
MB = 8
TOKENS = 128
N_SECTION = 64
N_DP = 8


def shard_levels(rng, extent, split, least, largest):
    def one(axis_at, shards_of):
        heights = jax.random.uniform(jax.random.fold_in(jax.random.fold_in(rng, 6), axis_at), (shards_of,), jnp.float32, least / len(split), largest / len(split))
        return jnp.repeat(jnp.exp(heights), extent[axis_at] // shards_of).reshape((-1,) + (1,) * (len(extent) - axis_at - 1))

    level = one(*split[0])
    for cut in split[1:]:
        level = level * one(*cut)
    return level


def gaussian(own_key, shape, spread, most, cuts=(), held_as=jnp.bfloat16):
    drawn = spread * jax.random.normal(own_key, shape, jnp.float32)
    if cuts:
        drawn = drawn * shard_levels(own_key, shape, cuts, -0.22, 0.18)
    return jnp.clip(drawn, -most, most).astype(held_as)


def setup_inputs(seed: int = 0) -> dict:
    key_of = jax.random.split(jax.random.key(seed), 5)
    return {
        "inputs": gaussian(key_of[0], (MB, TOKENS, D), 1.0, 6.0, ((1, 8), (2, 64))),
        "gain": jnp.clip(1.0 + 0.18 * jax.random.normal(key_of[1], (N_SECTION, D), jnp.float32), 0.1, 1.9),
        "w_in": gaussian(key_of[2], (N_SECTION, D, HD), D ** -0.5, 0.0625, ((0, 64),)),
        "w_out": gaussian(key_of[3], (N_SECTION, HD, D), HD ** -0.5, 0.5, ((0, 64),)),
    }


epsilon = 1e-05

def section_forward(inputs, gain_row, w_first, w_second):
    hidden = inputs.astype(jnp.float32)
    inverse = lax.rsqrt(lax.optimization_barrier(jnp.mean(hidden * hidden, axis=-1, keepdims=True)) + epsilon)
    normed = (hidden * inverse * gain_row).astype(jnp.bfloat16)
    project = jnp.dot(normed, w_first, preferred_element_type=jnp.float32)
    active = jax.nn.silu(project).astype(jnp.bfloat16)
    result = hidden + jnp.dot(active, w_second, preferred_element_type=jnp.float32)
    return (hidden, inverse, normed, project, active, result)

def section_backward(inputs, incoming, is_last, gain_row, w_first, w_second):
    hidden, inverse, normed, project, active, result = section_forward(inputs, gain_row, w_first, w_second)
    cotangent = jnp.where(is_last, result.astype(jnp.bfloat16), incoming)
    upper = jnp.dot(cotangent, w_second.T, preferred_element_type=jnp.float32)
    sigma = jax.nn.sigmoid(project)
    grad_project = (upper * sigma * (1.0 + project * (1.0 - sigma))).astype(jnp.bfloat16)
    grad_normed = jnp.dot(grad_project, w_first.T, preferred_element_type=jnp.float32)
    scaled = grad_normed * gain_row
    grad_hidden = cotangent.astype(jnp.float32) + inverse * scaled - hidden * inverse ** 3 * lax.optimization_barrier(jnp.mean(hidden * scaled, axis=-1, keepdims=True))
    return (grad_hidden.astype(jnp.bfloat16), normed, active, grad_project, cotangent)

def replica_sum(left, right, replicas, scale):
    left = left.reshape(replicas, -1, left.shape[-1]).astype(jnp.float32)
    right = right.reshape(replicas, -1, right.shape[-1]).astype(jnp.float32)
    parts = jnp.einsum('prd,prk->pdk', left, right)
    rounded = lax.optimization_barrier(parts.astype(jnp.bfloat16)).astype(jnp.float32)
    return (lax.optimization_barrier(jnp.sum(rounded, axis=0)) * scale).astype(jnp.bfloat16)

def reference(inputs, gain, w_in, w_out):
    sections = w_in.shape[0]
    micro, all_rows, width = inputs.shape
    replicas = N_DP
    per_rows = all_rows // replicas
    current = inputs.reshape(micro, replicas, per_rows, width).transpose(1, 0, 2, 3).reshape(replicas * micro * per_rows, width)
    saved = []
    for section_index in range(sections):
        saved.append(current)
        current = section_forward(current, gain[section_index], w_in[section_index], w_out[section_index])[5].astype(jnp.bfloat16)
    scale = 1.0 / math.sqrt(replicas * micro * per_rows)
    incoming = jnp.zeros_like(current)
    firsts = []
    seconds = []
    for section_index in range(sections - 1, -1, -1):
        sent, normed, active, grad_project, cotangent = section_backward(saved[section_index], incoming, section_index == sections - 1, gain[section_index], w_in[section_index], w_out[section_index])
        firsts.append(replica_sum(normed, grad_project, replicas, scale))
        seconds.append(replica_sum(cotangent, active, replicas, scale).T)
        incoming = sent
    grad_in = jnp.stack(firsts[::-1], axis=0)
    grad_out = jnp.stack(seconds[::-1], axis=0)
    return (grad_in, grad_out)
```

```python
import functools
import math

import jax
import jax.numpy as jnp
from jax import lax
from jax.experimental import pallas as pl
from jax.experimental.pallas import tpu as pltpu
from jax.sharding import Mesh, PartitionSpec as P

epsilon = 1e-05
f32 = jnp.float32
bf16 = jnp.bfloat16

D = 8192
HD = 128
LAYERS = 8
ROWS = 16
PARTS = 8
SLICE = D // PARTS
WIDE = SLICE + HD
SLOTS = 4
AHEAD = 3
NT = (((1,), (1,)), ((), ()))


def fetch_weights(place, pieces_in, pieces_out, held_in, held_out, sems, layer):
    slot = lax.rem(layer, SLOTS)
    apart = lax.rem(layer // 2 - place[1] + 4, 4)
    other = (lax.rem(layer, 2) != place[2]).astype(jnp.int32)
    which = apart * 2 + other
    for index in range(8):

        @pl.when(which == index)
        def _():
            pltpu.make_async_copy(pieces_in[index], held_in.at[slot], sems.at[0, slot]).start()
            pltpu.make_async_copy(pieces_out[index], held_out.at[slot], sems.at[1, slot]).start()


def forward_kernel(tick, place, x_ref, gain_ref, *refs):
    pieces_in, pieces_out = refs[:8], refs[8:16]
    (_, _, sent_ref, stash_ref, small_ref) = refs[16:21]
    (held_in, held_out, hidden, scaled, wide, small, sems, out_sems) = refs[21:]

    @pl.when(place[0] == tick)
    def _():
        for layer in range(AHEAD):
            fetch_weights(place, pieces_in, pieces_out, held_in, held_out, sems, jnp.int32(layer))
        hidden[...] = x_ref[...].astype(f32)

        def step(layer, carry):
            slot = lax.rem(layer, SLOTS)

            @pl.when(layer + AHEAD < LAYERS)
            def _():
                fetch_weights(place, pieces_in, pieces_out, held_in, held_out, sems, layer + AHEAD)

            squares = jnp.zeros((ROWS, 128), f32)
            for part in range(PARTS):
                lanes = slice(part * SLICE, (part + 1) * SLICE)
                value = hidden[:, lanes]
                wide[layer, part, :, :SLICE] = value.astype(bf16)
                scaled[:, lanes] = (value * gain_ref[pl.ds(layer, 1), lanes]).astype(bf16)
                square = value * value
                for at in range(0, SLICE, 128):
                    squares = squares + square[:, at : at + 128]
            inverse = lax.rsqrt(jnp.sum(squares, axis=-1, keepdims=True) * (1.0 / D) + epsilon)
            pltpu.make_async_copy(pieces_in[0], held_in.at[slot], sems.at[0, slot]).wait()
            project = inverse * jnp.dot(
                scaled[...], held_in[slot], preferred_element_type=f32
            )
            active = (project * jax.nn.sigmoid(project)).astype(bf16)
            small[layer, 0] = project
            small[layer, 1] = jnp.broadcast_to(inverse, (ROWS, HD))
            for part in range(PARTS):
                wide[layer, part, :, SLICE:] = active
            pltpu.make_async_copy(wide.at[layer], stash_ref.at[layer], out_sems.at[layer]).start()
            pltpu.make_async_copy(pieces_out[0], held_out.at[slot], sems.at[1, slot]).wait()
            for at in range(0, D, 512):
                hidden[:, at : at + 512] += jnp.dot(
                    active, held_out[slot, :, at : at + 512], preferred_element_type=f32
                )
            return carry

        lax.fori_loop(0, LAYERS, step, 0)
        last = pltpu.make_async_copy(small, small_ref, out_sems.at[LAYERS])
        last.start()
        sent_ref[...] = hidden[...].astype(bf16)
        for layer in range(LAYERS):
            pltpu.make_async_copy(wide.at[layer], stash_ref.at[layer], out_sems.at[layer]).wait()
        last.wait()


def backward_kernel(tick, place, c_ref, gain_ref, *refs):
    pieces_in, pieces_out = refs[:8], refs[8:16]
    (stash_ref, small_in, _, sent_ref, stash_out) = refs[16:21]
    (held_in, held_out, cotangent, rounded, stash, wide, small, sems, in_sems, out_sems) = refs[21:]

    @pl.when(place[0] == tick)
    def _():
        first = pltpu.make_async_copy(small_in, small, in_sems.at[LAYERS])
        first.start()
        for back in range(AHEAD):
            layer = LAYERS - 1 - back
            fetch_weights(place, pieces_in, pieces_out, held_in, held_out, sems, jnp.int32(layer))
        for back in range(LAYERS):
            layer = LAYERS - 1 - back
            pltpu.make_async_copy(stash_ref.at[layer], stash.at[layer], in_sems.at[layer]).start()
        cotangent[...] = c_ref[...].astype(f32)
        first.wait()

        def step(back, carry):
            layer = LAYERS - 1 - back
            slot = lax.rem(layer, SLOTS)

            @pl.when(layer - AHEAD >= 0)
            def _():
                fetch_weights(place, pieces_in, pieces_out, held_in, held_out, sems, layer - AHEAD)

            for part in range(PARTS):
                lanes = slice(part * SLICE, (part + 1) * SLICE)
                value = cotangent[:, lanes].astype(bf16)
                rounded[:, lanes] = value
                wide[layer, part, :, :SLICE] = value
            pltpu.make_async_copy(pieces_out[0], held_out.at[slot], sems.at[1, slot]).wait()
            upper = lax.dot_general(
                rounded[...], held_out[slot], NT, preferred_element_type=f32
            )
            project = small[layer, 0]
            inverse = small[layer, 1]
            sigma = jax.nn.sigmoid(project)
            slope = upper * sigma * (1.0 + project * (1.0 - sigma))
            factor = (slope * inverse).astype(bf16)
            for part in range(PARTS):
                wide[layer, part, :, SLICE:] = factor
            pltpu.make_async_copy(wide.at[layer], stash_out.at[layer], out_sems.at[layer]).start()
            inner = jnp.sum(slope * project, axis=-1, keepdims=True) * (1.0 / D)
            inner = inner * inverse[:, :1] * inverse[:, :1]
            pltpu.make_async_copy(stash_ref.at[layer], stash.at[layer], in_sems.at[layer]).wait()
            pltpu.make_async_copy(pieces_in[0], held_in.at[slot], sems.at[0, slot]).wait()
            for part in range(PARTS):
                for at in range(0, SLICE, 512):
                    start = part * SLICE + at
                    lanes = slice(start, start + 512)
                    grad = lax.dot_general(
                        factor, held_in[slot, lanes, :], NT, preferred_element_type=f32
                    )
                    hidden = stash[layer, part, :, at : at + 512].astype(f32)
                    cotangent[:, lanes] += (
                        grad * gain_ref[pl.ds(layer, 1), lanes] - hidden * inner
                    )
            return carry

        lax.fori_loop(0, LAYERS, step, 0)
        sent_ref[...] = cotangent[...].astype(bf16)
        for layer in range(LAYERS):
            pltpu.make_async_copy(wide.at[layer], stash_out.at[layer], out_sems.at[layer]).wait()


STASH = jax.ShapeDtypeStruct((LAYERS, PARTS, ROWS, WIDE), bf16)
SMALL = jax.ShapeDtypeStruct((LAYERS, 2, ROWS, HD), f32)
SENT = jax.ShapeDtypeStruct((ROWS, D), bf16)
ANY = pl.BlockSpec(memory_space=pl.ANY)
VMEM = pl.BlockSpec(memory_space=pltpu.VMEM)
SMEM = pl.BlockSpec(memory_space=pltpu.SMEM)
HELD = [
    pltpu.VMEM((SLOTS, D, HD), bf16),
    pltpu.VMEM((SLOTS, HD, D), bf16),
    pltpu.VMEM((ROWS, D), f32),
    pltpu.VMEM((ROWS, D), bf16),
]
PARAMS = pltpu.CompilerParams(vmem_limit_bytes=40 * 2**20)


def run_forward(tick, place, x, gains, pieces_in, pieces_out, stash, small):
    return pl.pallas_call(
        functools.partial(forward_kernel, tick),
        in_specs=[SMEM, VMEM, VMEM] + [ANY] * 18,
        out_specs=[VMEM, ANY, ANY],
        out_shape=[SENT, STASH, SMALL],
        input_output_aliases={19: 1, 20: 2},
        scratch_shapes=HELD
        + [
            pltpu.VMEM(STASH.shape, bf16),
            pltpu.VMEM(SMALL.shape, f32),
            pltpu.SemaphoreType.DMA((2, SLOTS)),
            pltpu.SemaphoreType.DMA((LAYERS + 1,)),
        ],
        compiler_params=PARAMS,
        name="team_forward",
    )(place, x, gains, *pieces_in, *pieces_out, stash, small)


def run_backward(tick, place, c, gains, pieces_in, pieces_out, stash, small, cots):
    return pl.pallas_call(
        functools.partial(backward_kernel, tick),
        in_specs=[SMEM, VMEM, VMEM] + [ANY] * 19,
        out_specs=[VMEM, ANY],
        out_shape=[SENT, STASH],
        input_output_aliases={21: 1},
        scratch_shapes=HELD
        + [
            pltpu.VMEM(STASH.shape, bf16),
            pltpu.VMEM(STASH.shape, bf16),
            pltpu.VMEM(SMALL.shape, f32),
            pltpu.SemaphoreType.DMA((2, SLOTS)),
            pltpu.SemaphoreType.DMA((LAYERS + 1,)),
            pltpu.SemaphoreType.DMA((LAYERS,)),
        ],
        compiler_params=PARAMS,
        name="team_backward",
    )(place, c, gains, *pieces_in, *pieces_out, stash, small, cots)


def along_z(value, steps):
    index = [(z % 4) * 2 + z // 4 for z in range(8)]
    pairs = [(index[z], index[(z + steps) % 8]) for z in range(8)]
    return lax.ppermute(value, ("zl", "zh"), pairs)


def swap_cores(value):
    return lax.ppermute(value, "core", [(0, 1), (1, 0)])


def along_y(value, source, target):
    return lax.ppermute(value, "y", [(source, target)])


PLANE = ("zl", "core", "x", "zh")


def exchange(stash):
    flat = stash.reshape(LAYERS * PARTS, ROWS, WIDE)
    flat = lax.all_to_all(flat, PLANE, 0, 0, tiled=True)
    return flat.reshape(LAYERS * PARTS * ROWS, WIDE)


def local(inputs, gain, w_in, w_out):
    y = lax.axis_index("y")
    place = jnp.stack([y, lax.axis_index("zl"), lax.axis_index("core")]).astype(jnp.int32)
    own_in, own_out = w_in[0], w_out[0]
    before_in, after_out = along_z(own_in, 1), along_z(own_out, -1)
    before_out, after_in = along_z(own_out, 1), along_z(own_in, -1)
    far_in, far_out = along_z(before_in, 1), along_z(after_out, -1)
    pieces_in = [own_in, swap_cores(own_in), after_in, swap_cores(after_in)]
    pieces_in += [far_in, swap_cores(far_in), before_in, swap_cores(before_in)]
    pieces_out = [own_out, swap_cores(own_out), after_out, swap_cores(after_out)]
    pieces_out += [far_out, swap_cores(far_out), before_out, swap_cores(before_out)]
    gains = lax.all_gather(gain, ("zl", "core"), axis=0, tiled=True)
    x = lax.all_to_all(inputs, ("zl", "core"), 0, 0, tiled=True)
    x = x.transpose(1, 0, 2).reshape(ROWS, SLICE)
    x = lax.all_gather(x, "y", axis=1, tiled=True)

    stash = jnp.zeros(STASH.shape, bf16)
    small = jnp.zeros(SMALL.shape, f32)
    for tick in range(8):
        x, stash, small = run_forward(tick, place, x, gains, pieces_in, pieces_out, stash, small)
        if tick < 7:
            x = along_y(x, tick, tick + 1)
    cots = jnp.zeros(STASH.shape, bf16)
    for tick in range(7, -1, -1):
        x, cots = run_backward(tick, place, x, gains, pieces_in, pieces_out, stash, small, cots)
        if tick > 0:
            x = along_y(x, tick, tick - 1)

    first = exchange(stash)
    second = exchange(cots)
    part = lax.axis_index("x") * 2 + lax.axis_index("zh")
    own_gain = lax.dynamic_slice(gain, (0, part * SLICE), (1, SLICE)).reshape(SLICE, 1)
    scale = 1.0 / math.sqrt(LAYERS * PARTS * ROWS)
    rows = (((0,), (0,)), ((), ()))
    sum_in = lax.dot_general(
        first[:, :SLICE], second[:, SLICE:], rows, preferred_element_type=f32
    )
    sum_out = lax.dot_general(
        first[:, SLICE:], second[:, :SLICE], rows, preferred_element_type=f32
    )
    grad_in = (sum_in * own_gain * scale).astype(bf16)[None]
    grad_out = (sum_out * scale).astype(bf16)[None]
    return (grad_in, grad_out)


def solution(mesh):
    axes = ("y", "zl", "core", "x", "zh")
    split = Mesh(mesh.devices.reshape(8, 4, 2, 4, 2), axes)
    section, replica = ("y", "zl", "core"), ("x", "zh")
    return jax.shard_map(
        local,
        mesh=split,
        in_specs=(
            P(None, replica, section),
            P(section, None),
            P(section, None, None),
            P(section, None, None),
        ),
        out_specs=(P(section, replica, None), P(section, None, replica)),
        check_vma=False,
    )
```

```python
import functools
import math

import jax
import jax.numpy as jnp
from jax import lax
from jax.experimental import pallas as pl
from jax.experimental.pallas import tpu as pltpu
from jax.sharding import Mesh, PartitionSpec as P

epsilon = 1e-05
f32 = jnp.float32
bf16 = jnp.bfloat16

D = 8192
HD = 128
LAYERS = 8
ROWS = 16
PARTS = 8
SLICE = D // PARTS
WIDE = SLICE + HD
LAST = 7
FIRST_EXCHANGE = 7
SLOTS = 4
AHEAD = 3
EARLY = 2


def fetch(place, pieces, held, sems, layer):
    layer = jnp.int32(layer)
    slot = lax.rem(layer, held.shape[0])
    apart = lax.rem(layer // 2 - place[1] + 4, 4)
    other = (lax.rem(layer, 2) != place[2]).astype(jnp.int32)
    which = apart * 2 + other
    for index in range(8):

        @pl.when(which == index)
        def _():
            pltpu.make_async_copy(pieces[index], held.at[slot], sems.at[slot]).start()


def await_fetch(pieces, held, sems, layer):
    slot = lax.rem(jnp.int32(layer), held.shape[0])
    pltpu.make_async_copy(pieces[0], held.at[slot], sems.at[slot]).wait()
    return slot


def forward_pass(refs, fetches, get_in, get_out):
    x_ref, sent_ref, stash_ref, small_ref = refs[:4]
    hidden, narrow, wide, small, out_sems = refs[4:]
    for layer in range(AHEAD):
        fetches(layer)
    hidden[...] = x_ref[...].astype(f32)

    def step(layer, carry):
        @pl.when(layer + AHEAD < LAYERS)
        def _():
            fetches(layer + AHEAD)

        squares = jnp.zeros((ROWS, 128), f32)
        for part in range(PARTS):
            lanes = slice(part * SLICE, (part + 1) * SLICE)
            value = hidden[:, lanes]
            wide[layer, part, :, :SLICE] = value.astype(bf16)
            narrow[:, lanes] = value.astype(bf16)
            square = value * value
            for at in range(0, SLICE, 128):
                squares = squares + square[:, at : at + 128]
        inverse = lax.rsqrt(jnp.sum(squares, axis=-1, keepdims=True) * (1.0 / D) + epsilon)
        weights = get_in(layer)
        project = inverse * jnp.dot(narrow[...], weights[...], preferred_element_type=f32)
        active = (project * jax.nn.sigmoid(project)).astype(bf16)
        small[layer, 0] = project
        small[layer, 1] = jnp.broadcast_to(inverse, (ROWS, HD))
        for part in range(PARTS):
            wide[layer, part, :, SLICE:] = active
        pltpu.make_async_copy(wide.at[layer], stash_ref.at[layer], out_sems.at[layer]).start()
        weights = get_out(layer)
        for at in range(0, D, 512):
            hidden[:, at : at + 512] += jnp.dot(
                active, weights[:, at : at + 512], preferred_element_type=f32
            )
        return carry

    lax.fori_loop(0, LAYERS, step, 0)
    last = pltpu.make_async_copy(small, small_ref, out_sems.at[LAYERS])
    last.start()
    sent_ref[...] = hidden[...].astype(bf16)
    for layer in range(LAYERS):
        pltpu.make_async_copy(wide.at[layer], stash_ref.at[layer], out_sems.at[layer]).wait()
    last.wait()


def early_kernel(tick, place, x_ref, *refs):
    pieces_in, pieces_out = refs[:8], refs[8:16]
    refs = refs[16:] if tick == 0 else refs[18:]
    state, (held_in, held_out, in_sems, held_sems) = refs[3:8], refs[8:]

    @pl.when(place[0] == tick)
    def _():
        def fetches(layer):
            fetch(place, pieces_in, held_in, in_sems, layer)
            fetch(place, pieces_out, held_out, held_sems, layer)

        forward_pass(
            (x_ref,) + tuple(refs[:3]) + tuple(state),
            fetches,
            lambda layer: held_in.at[await_fetch(pieces_in, held_in, in_sems, layer)],
            lambda layer: held_out.at[await_fetch(pieces_out, held_out, held_sems, layer)],
        )


def forward_kernel(tick, place, x_ref, held_out, *refs):
    pieces_in, refs = refs[:8], refs[10:]
    state, (held_in, in_sems) = refs[3:8], refs[8:]

    @pl.when(place[0] == tick)
    def _():
        forward_pass(
            (x_ref,) + tuple(refs[:3]) + tuple(state),
            lambda layer: fetch(place, pieces_in, held_in, in_sems, layer),
            lambda layer: held_in.at[await_fetch(pieces_in, held_in, in_sems, layer)],
            lambda layer: held_out.at[layer],
        )


def load_kernel(place, *refs):
    pieces_out, pieces_in = refs[:8], refs[8:16]
    held_out, turned_out, turned_in = refs[17:20]
    first, second, last, sems, in_sem, out_sems, last_sem = refs[20:]
    for layer in range(LAYERS):
        fetch(place, pieces_out, held_out, sems, layer)
    fetch(place, pieces_in, last, in_sem, LAYERS - 1)

    def step(layer, carry):
        slot = lax.rem(layer, 2)
        copy = pltpu.make_async_copy(first.at[slot], turned_out.at[layer], out_sems.at[slot])

        @pl.when(layer >= 2)
        def _():
            copy.wait()

        await_fetch(pieces_out, held_out, sems, layer)
        for at in range(0, D, HD):
            first[slot, at : at + HD, :] = held_out[layer, :, at : at + HD].T
        copy.start()
        return carry

    lax.fori_loop(0, LAYERS, step, 0)
    await_fetch(pieces_in, last, in_sem, 0)
    for at in range(0, D, HD):
        second[:, at : at + HD] = last[0, at : at + HD, :].T
    copy = pltpu.make_async_copy(second, turned_in, last_sem.at[0])
    copy.start()
    for layer in range(LAYERS - 2, LAYERS):
        pltpu.make_async_copy(
            first.at[layer % 2], turned_out.at[layer], out_sems.at[layer % 2]
        ).wait()
    copy.wait()


def backward_layer(layer, refs, first, second, extra):
    (stash_ref, stash_out, cotangent, rounded, stash, wide, small, in_sems, out_sems) = refs
    for part in range(PARTS):
        lanes = slice(part * SLICE, (part + 1) * SLICE)
        value = cotangent[:, lanes].astype(bf16)
        rounded[:, lanes] = value
        wide[layer, part, :, :SLICE] = value
    pltpu.make_async_copy(stash_ref.at[layer], stash.at[layer], in_sems.at[layer]).wait()
    upper = jnp.dot(rounded[...], first(), preferred_element_type=f32)
    extra()
    project = small[layer, 0]
    inverse = small[layer, 1]
    sigma = jax.nn.sigmoid(project)
    slope = upper * sigma * (1.0 + project * (1.0 - sigma))
    factor = (slope * inverse).astype(bf16)
    for part in range(PARTS):
        wide[layer, part, :, SLICE:] = factor
    inner = jnp.sum(slope * project, axis=-1, keepdims=True) * (1.0 / D)
    inner = inner * inverse[:, :1] * inverse[:, :1]
    for part in range(PARTS):
        for at in range(0, SLICE, 512):
            lanes = slice(part * SLICE + at, part * SLICE + at + 512)
            grad = jnp.dot(factor, second(lanes), preferred_element_type=f32)
            hidden = stash[layer, part, :, at : at + 512].astype(f32)
            cotangent[:, lanes] += grad - hidden * inner
    pltpu.make_async_copy(wide.at[layer], stash_out.at[layer], out_sems.at[layer]).start()


def backward_kernel(tick, place, c_ref, turned_out, turned_in, *refs):
    pieces_in, stash_ref, small_in = refs[:8], refs[8], refs[9]
    refs = refs[10:] if tick == LAST else refs[11:]
    sent_ref, stash_out = refs[:2]
    (cotangent, rounded, stash, wide, small, in_sems, out_sems, held_in, held_sems) = refs[2:11]
    first, first_sems, last_sem = refs[11:14]
    seconds = refs[14:16]
    common = (
        stash_ref, stash_out, cotangent, rounded, stash, wide, small, in_sems, out_sems,
    )

    def fetch_turned(layer):
        slot = lax.rem(layer, SLOTS)
        return pltpu.make_async_copy(turned_out.at[layer], first.at[slot], first_sems.at[slot])

    def turn(layer, second):
        slot = lax.rem(layer, SLOTS)
        for at in range(0, D, HD):
            second[:, at : at + HD] = held_in[slot, at : at + HD, :].T

    def one_layer(layer, now, later):
        @pl.when((layer >= SLOTS - 1) & (layer < LAYERS - 1))
        def _():
            fetch_turned(layer - SLOTS + 1).start()

        @pl.when(layer >= SLOTS)
        def _():
            fetch(place, pieces_in, held_in, held_sems, layer - SLOTS)

        @pl.when(layer > 0)
        def _():
            await_fetch(pieces_in, held_in, held_sems, layer - 1)

        fetch_turned(layer).wait()
        backward_layer(
            layer,
            common,
            lambda: first[lax.rem(layer, SLOTS)],
            lambda lanes: now[:, lanes],
            lambda: turn(jnp.maximum(layer - 1, 0), later),
        )

    @pl.when(place[0] == tick)
    def _():
        start = pltpu.make_async_copy(small_in, small, in_sems.at[LAYERS])
        start.start()
        fetch_turned(jnp.int32(LAYERS - 1)).start()
        last = pltpu.make_async_copy(turned_in, seconds[0], last_sem.at[0])
        last.start()

        def begin(back, carry):
            layer = LAYERS - 1 - back
            pltpu.make_async_copy(stash_ref.at[layer], stash.at[layer], in_sems.at[layer]).start()

            @pl.when((back > 0) & (back < SLOTS))
            def _():
                fetch(place, pieces_in, held_in, held_sems, layer)
                fetch_turned(layer).start()

            return carry

        lax.fori_loop(0, LAYERS, begin, 0)
        cotangent[...] = c_ref[...].astype(f32)
        start.wait()
        last.wait()

        def two_layers(back, carry):
            layer = LAYERS - 1 - 2 * back
            one_layer(layer, seconds[0], seconds[1])
            one_layer(layer - 1, seconds[1], seconds[0])
            return carry

        lax.fori_loop(0, LAYERS // 2, two_layers, 0)
        sent_ref[...] = cotangent[...].astype(bf16)

        def end(layer, carry):
            pltpu.make_async_copy(wide.at[layer], stash_out.at[layer], out_sems.at[layer]).wait()
            return carry

        lax.fori_loop(0, LAYERS, end, 0)


STASH = jax.ShapeDtypeStruct((LAYERS, PARTS, ROWS, WIDE), bf16)
SMALL = jax.ShapeDtypeStruct((LAYERS, 2, ROWS, HD), f32)
SENT = jax.ShapeDtypeStruct((ROWS, D), bf16)
ANY = pl.BlockSpec(memory_space=pl.ANY)
VMEM = pl.BlockSpec(memory_space=pltpu.VMEM)
SMEM = pl.BlockSpec(memory_space=pltpu.SMEM)
STATE = [pltpu.VMEM((ROWS, D), f32), pltpu.VMEM((ROWS, D), bf16)]
PARAMS = pltpu.CompilerParams(vmem_limit_bytes=30 * 2**20)


COST = pl.CostEstimate(flops=4 * LAYERS * ROWS * D * HD, bytes_accessed=36 * 2**20, transcendentals=0)


def in_hbm(value):
    return pltpu.with_memory_space_constraint(value, pltpu.HBM)


def in_vmem(value):
    return pltpu.with_memory_space_constraint(value, pltpu.VMEM)


STREAM_IN = [pltpu.VMEM((SLOTS, D, HD), bf16), pltpu.SemaphoreType.DMA((SLOTS,))]
FORWARD = STATE + [
    pltpu.VMEM(STASH.shape, bf16),
    pltpu.VMEM(SMALL.shape, f32),
    pltpu.SemaphoreType.DMA((LAYERS + 1,)),
]


def run_load(place, pieces_in, pieces_out, after):
    return pl.pallas_call(
        load_kernel,
        in_specs=[SMEM] + [ANY] * 17,
        out_specs=[VMEM, ANY, ANY],
        out_shape=[
            pltpu.VMEM((LAYERS, HD, D), bf16),
            jax.ShapeDtypeStruct((LAYERS, D, HD), bf16),
            jax.ShapeDtypeStruct((HD, D), bf16),
        ],
        scratch_shapes=[
            pltpu.VMEM((2, D, HD), bf16),
            pltpu.VMEM((HD, D), bf16),
            pltpu.VMEM((1, D, HD), bf16),
            pltpu.SemaphoreType.DMA((LAYERS,)),
            pltpu.SemaphoreType.DMA((1,)),
            pltpu.SemaphoreType.DMA((2,)),
            pltpu.SemaphoreType.DMA((1,)),
        ],
        compiler_params=pltpu.CompilerParams(vmem_limit_bytes=10 * 2**20),
        cost_estimate=COST,
        name="team_load",
    )(place, *map(in_hbm, pieces_out), *map(in_hbm, pieces_in), after)


def run_early(tick, place, x, pieces_in, pieces_out, stash, small):
    older = [] if stash is None else [stash, small]
    return pl.pallas_call(
        functools.partial(early_kernel, tick),
        in_specs=[SMEM, VMEM] + [ANY] * (16 + len(older)),
        out_specs=[VMEM, ANY, ANY],
        out_shape=[SENT, STASH, SMALL],
        input_output_aliases={18: 1, 19: 2} if older else {},
        scratch_shapes=FORWARD
        + [
            pltpu.VMEM((SLOTS, D, HD), bf16),
            pltpu.VMEM((SLOTS, HD, D), bf16),
            pltpu.SemaphoreType.DMA((SLOTS,)),
            pltpu.SemaphoreType.DMA((SLOTS,)),
        ],
        compiler_params=PARAMS,
        cost_estimate=COST,
        name="team_early",
    )(place, x, *map(in_hbm, pieces_in), *map(in_hbm, pieces_out), *map(in_hbm, older))


def run_forward(tick, place, x, held_out, pieces_in, stash, small):
    return pl.pallas_call(
        functools.partial(forward_kernel, tick),
        in_specs=[SMEM, VMEM, VMEM] + [ANY] * 10,
        out_specs=[VMEM, ANY, ANY],
        out_shape=[SENT, STASH, SMALL],
        input_output_aliases={11: 1, 12: 2},
        scratch_shapes=FORWARD + STREAM_IN,
        compiler_params=PARAMS,
        cost_estimate=COST,
        name="team_forward",
    )(place, x, in_vmem(held_out), *map(in_hbm, pieces_in), in_hbm(stash), in_hbm(small))


def run_backward(tick, place, c, turned_out, turned_in, pieces_in, stash, small, cots):
    older = [] if cots is None else [cots]
    return pl.pallas_call(
        functools.partial(backward_kernel, tick),
        in_specs=[SMEM, VMEM] + [ANY] * (12 + len(older)),
        out_specs=[VMEM, ANY],
        out_shape=[SENT, STASH],
        input_output_aliases={14: 1} if older else {},
        scratch_shapes=STATE
        + [
            pltpu.VMEM(STASH.shape, bf16),
            pltpu.VMEM(STASH.shape, bf16),
            pltpu.VMEM(SMALL.shape, f32),
            pltpu.SemaphoreType.DMA((LAYERS + 1,)),
            pltpu.SemaphoreType.DMA((LAYERS,)),
        ]
        + STREAM_IN
        + STREAM_IN
        + [pltpu.SemaphoreType.DMA((1,)), pltpu.VMEM((HD, D), bf16), pltpu.VMEM((HD, D), bf16)],
        compiler_params=PARAMS,
        cost_estimate=COST,
        name="team_backward",
    )(place, c, *map(in_hbm, [turned_out, turned_in, *pieces_in, stash, small, *older]))


def along_z(value, steps):
    index = [(z % 4) * 2 + z // 4 for z in range(8)]
    pairs = [(index[z], index[(z + steps) % 8]) for z in range(8)]
    return lax.ppermute(value, ("zl", "zh"), pairs)


def swap_cores(value):
    return lax.ppermute(value, "core", [(0, 1), (1, 0)])


def along_y(value, source, target):
    return lax.ppermute(value, "y", [(source, target)])


PLANE = ("zl", "core", "x", "zh")


def exchange(stash):
    flat = stash.reshape(LAYERS * PARTS, ROWS, WIDE)
    flat = lax.all_to_all(flat, PLANE, 0, 0, tiled=True)
    return flat.reshape(LAYERS * PARTS * ROWS, WIDE)


def local(inputs, gain, w_in, w_out):
    axes = ("y", "zl", "core")
    place = jnp.stack([lax.axis_index(axis) for axis in axes]).astype(jnp.int32)
    own_in, own_out = w_in[0], w_out[0]
    own_in = (own_in.astype(f32) * gain[0][:, None]).astype(bf16)
    before_in, after_out = along_z(own_in, 1), along_z(own_out, -1)
    before_out, after_in = along_z(own_out, 1), along_z(own_in, -1)
    near_in, near_out, inputs = lax.optimization_barrier((before_in, after_out, inputs))
    far_in, far_out = along_z(near_in, 1), along_z(near_out, -1)
    x = jnp.broadcast_to(inputs, (8,) + inputs.shape).reshape(64, ROWS, HD)
    x = lax.all_to_all(x, ("y", "zl", "core"), 0, 0, tiled=True)
    x = x.transpose(1, 0, 2).reshape(ROWS, D)
    (before_out, after_in, x) = lax.optimization_barrier((before_out, after_in, x))
    pieces_in = [own_in, swap_cores(own_in), after_in, swap_cores(after_in)]
    pieces_in += [far_in, swap_cores(far_in), near_in, swap_cores(near_in)]
    pieces_out = [own_out, swap_cores(own_out), near_out, swap_cores(near_out)]
    pieces_out += [far_out, swap_cores(far_out), before_out, swap_cores(before_out)]

    stash = small = cots = None
    for tick in range(8):
        if tick > 0:
            last, x = x, along_y(x, tick - 1, tick)
        if tick < EARLY:
            x, stash, small = run_early(tick, place, x, pieces_in, pieces_out, stash, small)
            continue
        if tick == EARLY:
            held_out, turned_out, turned_in = run_load(place, pieces_in, pieces_out, last)
        x, stash, small = run_forward(tick, place, x, held_out, pieces_in, stash, small)
    for tick in range(LAST, -1, -1):
        if tick < LAST:
            x = along_y(x, tick + 1, tick)
        x, cots = run_backward(
            tick, place, x, turned_out, turned_in, pieces_in, stash, small, cots
        )
        if tick == FIRST_EXCHANGE:
            x, stash_sent = lax.optimization_barrier((x, stash))
            first = exchange(stash_sent)

    second = exchange(cots)
    part = lax.axis_index("x") * 2 + lax.axis_index("zh")
    own_gain = lax.dynamic_slice(gain, (0, part * SLICE), (1, SLICE)).reshape(SLICE, 1)
    scale = 1.0 / math.sqrt(LAYERS * PARTS * ROWS)
    rows = (((0,), (0,)), ((), ()))
    sum_in = lax.dot_general(
        first[:, :SLICE], second[:, SLICE:], rows, preferred_element_type=f32
    )
    sum_out = lax.dot_general(
        first[:, SLICE:], second[:, :SLICE], rows, preferred_element_type=f32
    )
    grad_in = (sum_in * own_gain * scale).astype(bf16)[None]
    grad_out = (sum_out * scale).astype(bf16)[None]
    return (grad_in, grad_out)


def solution(mesh):
    axes = ("y", "zl", "core", "x", "zh")
    split = Mesh(mesh.devices.reshape(8, 4, 2, 4, 2), axes)
    section, replica = ("y", "zl", "core"), ("x", "zh")
    return jax.shard_map(
        local,
        mesh=split,
        in_specs=(
            P(None, replica, section),
            P(section, None),
            P(section, None, None),
            P(section, None, None),
        ),
        out_specs=(P(section, replica, None), P(section, None, replica)),
        check_vma=False,
    )
```

```python
import functools
import math

import jax
import jax.numpy as jnp
from jax import lax
from jax.experimental import pallas as pl
from jax.experimental.pallas import tpu as pltpu
from jax.sharding import Mesh, PartitionSpec as P

epsilon = 1e-05
f32 = jnp.float32
bf16 = jnp.bfloat16

D = 8192
HD = 128
LAYERS = 8
ROWS = 16
PARTS = 8
SLICE = D // PARTS
WIDE = SLICE + HD
LAST = 7
SLOTS = 4
AHEAD = 3
EARLY = 1


def fetch(place, pieces, held, sems, layer):
    layer = jnp.int32(layer)
    slot = lax.rem(layer, held.shape[0])
    apart = lax.rem(layer // 2 - place[1] + 4, 4)
    other = (lax.rem(layer, 2) != place[2]).astype(jnp.int32)
    which = apart * 2 + other
    for index in range(8):

        @pl.when(which == index)
        def _():
            pltpu.make_async_copy(pieces[index], held.at[slot], sems.at[slot]).start()


def await_fetch(pieces, held, sems, layer):
    slot = lax.rem(jnp.int32(layer), held.shape[0])
    pltpu.make_async_copy(pieces[0], held.at[slot], sems.at[slot]).wait()
    return slot


def forward_pass(refs, fetches, get_in, get_out):
    x_ref, sent_ref, stash_ref, small_ref = refs[:4]
    hidden, narrow, wide, small, out_sems = refs[4:]
    for layer in range(AHEAD):
        fetches(layer)
    hidden[...] = x_ref[...].astype(f32)

    def step(layer, carry):
        @pl.when(layer + AHEAD < LAYERS)
        def _():
            fetches(layer + AHEAD)

        weights = get_in(layer)
        squares = jnp.zeros((ROWS, 128), f32)
        for part in range(PARTS):
            lanes = slice(part * SLICE, (part + 1) * SLICE)
            value = hidden[:, lanes]
            wide[layer, part, :, :SLICE] = value.astype(bf16)
            narrow[:, lanes] = value.astype(bf16)
            square = value * value
            for at in range(0, SLICE, 128):
                squares = squares + square[:, at : at + 128]
        inverse = lax.rsqrt(jnp.sum(squares, axis=-1, keepdims=True) * (1.0 / D) + epsilon)
        project = inverse * jnp.dot(narrow[...], weights[...], preferred_element_type=f32)
        active = (project * jax.nn.sigmoid(project)).astype(bf16)
        small[layer, 0] = project
        small[layer, 1] = jnp.broadcast_to(inverse, (ROWS, HD))
        for part in range(PARTS):
            wide[layer, part, :, SLICE:] = active
        pltpu.make_async_copy(wide.at[layer], stash_ref.at[layer], out_sems.at[layer]).start()
        weights = get_out(layer)
        for at in range(0, D, 512):
            hidden[:, at : at + 512] += jnp.dot(
                active, weights[:, at : at + 512], preferred_element_type=f32
            )
        return carry

    lax.fori_loop(0, LAYERS, step, 0)
    last = pltpu.make_async_copy(small, small_ref, out_sems.at[LAYERS])
    last.start()
    sent_ref[...] = hidden[...].astype(bf16)
    for layer in range(LAYERS):
        pltpu.make_async_copy(wide.at[layer], stash_ref.at[layer], out_sems.at[layer]).wait()
    last.wait()


def early_kernel(tick, place, x_ref, *refs):
    pieces_in, pieces_out = refs[:8], refs[8:16]
    refs = refs[16:] if tick == 0 else refs[18:]
    state, (held_in, held_out, in_sems, held_sems) = refs[3:8], refs[8:]

    @pl.when(place[0] == tick)
    def _():
        def fetches(layer):
            fetch(place, pieces_in, held_in, in_sems, layer)
            fetch(place, pieces_out, held_out, held_sems, layer)

        forward_pass(
            (x_ref,) + tuple(refs[:3]) + tuple(state),
            fetches,
            lambda layer: held_in.at[await_fetch(pieces_in, held_in, in_sems, layer)],
            lambda layer: held_out.at[await_fetch(pieces_out, held_out, held_sems, layer)],
        )


def forward_kernel(tick, place, x_ref, held_out, *refs):
    pieces_in, refs = refs[:8], refs[10:]
    state, (held_in, in_sems) = refs[3:8], refs[8:]

    @pl.when(place[0] == tick)
    def _():
        forward_pass(
            (x_ref,) + tuple(refs[:3]) + tuple(state),
            lambda layer: fetch(place, pieces_in, held_in, in_sems, layer),
            lambda layer: held_in.at[await_fetch(pieces_in, held_in, in_sems, layer)],
            lambda layer: held_out.at[layer],
        )


def load_kernel(place, *refs):
    pieces_out, pieces_in = refs[:8], refs[8:16]
    held_out, turned_out, turned_in = refs[17:20]
    first, second, last, sems, in_sem, out_sems, last_sem = refs[20:]
    for layer in range(LAYERS):
        fetch(place, pieces_out, held_out, sems, layer)
    fetch(place, pieces_in, last, in_sem, LAYERS - 1)

    def step(layer, carry):
        slot = lax.rem(layer, 2)
        copy = pltpu.make_async_copy(first.at[slot], turned_out.at[layer], out_sems.at[slot])

        @pl.when(layer >= 2)
        def _():
            copy.wait()

        await_fetch(pieces_out, held_out, sems, layer)
        for at in range(0, D, HD):
            first[slot, at : at + HD, :] = held_out[layer, :, at : at + HD].T
        copy.start()
        return carry

    lax.fori_loop(0, LAYERS, step, 0)
    await_fetch(pieces_in, last, in_sem, 0)
    for at in range(0, D, HD):
        second[:, at : at + HD] = last[0, at : at + HD, :].T
    copy = pltpu.make_async_copy(second, turned_in, last_sem.at[0])
    copy.start()
    for layer in range(LAYERS - 2, LAYERS):
        pltpu.make_async_copy(
            first.at[layer % 2], turned_out.at[layer], out_sems.at[layer % 2]
        ).wait()
    copy.wait()


def backward_layer(layer, refs, first, second, extra):
    (stash_ref, stash_out, cotangent, rounded, stash, wide, small, in_sems, out_sems) = refs
    for part in range(PARTS):
        lanes = slice(part * SLICE, (part + 1) * SLICE)
        value = cotangent[:, lanes].astype(bf16)
        rounded[:, lanes] = value
        wide[layer, part, :, :SLICE] = value
    upper = jnp.dot(rounded[...], first(), preferred_element_type=f32)
    extra()
    project = small[layer, 0]
    inverse = small[layer, 1]
    sigma = jax.nn.sigmoid(project)
    slope = upper * sigma * (1.0 + project * (1.0 - sigma))
    factor = (slope * inverse).astype(bf16)
    for part in range(PARTS):
        wide[layer, part, :, SLICE:] = factor
    inner = jnp.sum(slope * project, axis=-1, keepdims=True) * (1.0 / D)
    inner = inner * inverse[:, :1] * inverse[:, :1]
    for part in range(PARTS):
        for at in range(0, SLICE, 512):
            lanes = slice(part * SLICE + at, part * SLICE + at + 512)
            grad = jnp.dot(factor, second(lanes), preferred_element_type=f32)
            hidden = stash[layer, part, :, at : at + 512].astype(f32)
            cotangent[:, lanes] += grad - hidden * inner
    pltpu.make_async_copy(wide.at[layer], stash_out.at[layer], out_sems.at[layer]).start()


def backward_kernel(tick, place, c_ref, turned_out, turned_in, *refs):
    pieces_in, stash_ref, small_in = refs[:8], refs[8], refs[9]
    refs = refs[10:] if tick == LAST else refs[11:]
    sent_ref, stash_out = refs[:2]
    (cotangent, rounded, stash, wide, small, in_sems, out_sems, held_in, held_sems) = refs[2:11]
    last_sem, *seconds = refs[11:14]
    common = (
        stash_ref, stash_out, cotangent, rounded, stash, wide, small, in_sems, out_sems,
    )

    def turn(layer, second):
        slot = lax.rem(layer, SLOTS)
        for at in range(0, D, HD):
            second[:, at : at + HD] = held_in[slot, at : at + HD, :].T

    def one_layer(layer, now, later):
        @pl.when(layer >= SLOTS)
        def _():
            fetch(place, pieces_in, held_in, held_sems, layer - SLOTS)

        @pl.when(layer > 0)
        def _():
            await_fetch(pieces_in, held_in, held_sems, layer - 1)

        pltpu.make_async_copy(stash_ref.at[layer], stash.at[layer], in_sems.at[layer]).wait()
        backward_layer(
            layer,
            common,
            lambda: turned_out[layer],
            lambda lanes: now[:, lanes],
            lambda: turn(jnp.maximum(layer - 1, 0), later),
        )

    @pl.when(place[0] == tick)
    def _():
        start = pltpu.make_async_copy(small_in, small, in_sems.at[LAYERS])
        start.start()
        last = pltpu.make_async_copy(turned_in, seconds[0], last_sem.at[0])
        last.start()

        def begin(back, carry):
            layer = LAYERS - 1 - back
            pltpu.make_async_copy(stash_ref.at[layer], stash.at[layer], in_sems.at[layer]).start()

            @pl.when((back > 0) & (back < SLOTS))
            def _():
                fetch(place, pieces_in, held_in, held_sems, layer)

            return carry

        lax.fori_loop(0, LAYERS, begin, 0)
        cotangent[...] = c_ref[...].astype(f32)
        start.wait()
        last.wait()

        def two_layers(back, carry):
            layer = LAYERS - 1 - 2 * back
            one_layer(layer, seconds[0], seconds[1])
            one_layer(layer - 1, seconds[1], seconds[0])
            return carry

        lax.fori_loop(0, LAYERS // 2, two_layers, 0)
        sent_ref[...] = cotangent[...].astype(bf16)

        def end(layer, carry):
            pltpu.make_async_copy(wide.at[layer], stash_out.at[layer], out_sems.at[layer]).wait()
            return carry

        lax.fori_loop(0, LAYERS, end, 0)


STASH = pltpu.HBM((LAYERS, PARTS, ROWS, WIDE), bf16)
SMALL = pltpu.HBM((LAYERS, 2, ROWS, HD), f32)
SENT = jax.ShapeDtypeStruct((ROWS, D), bf16)
ANY = pl.BlockSpec(memory_space=pl.ANY)
VMEM = pl.BlockSpec(memory_space=pltpu.VMEM)
SMEM = pl.BlockSpec(memory_space=pltpu.SMEM)
STATE = [pltpu.VMEM((ROWS, D), f32), pltpu.VMEM((ROWS, D), bf16)]
PARAMS = pltpu.CompilerParams(vmem_limit_bytes=20 * 2**20)


COST = pl.CostEstimate(flops=4 * LAYERS * ROWS * D * HD, bytes_accessed=36 * 2**20, transcendentals=0)


def in_hbm(value):
    return pltpu.with_memory_space_constraint(value, pltpu.HBM)


def in_vmem(value):
    return pltpu.with_memory_space_constraint(value, pltpu.VMEM)


STREAM_IN = [pltpu.VMEM((SLOTS, D, HD), bf16), pltpu.SemaphoreType.DMA((SLOTS,))]
FORWARD = STATE + [
    pltpu.VMEM(STASH.shape, bf16),
    pltpu.VMEM(SMALL.shape, f32),
    pltpu.SemaphoreType.DMA((LAYERS + 1,)),
]


def run_load(place, pieces_in, pieces_out, after):
    return pl.pallas_call(
        load_kernel,
        in_specs=[SMEM] + [ANY] * 17,
        out_specs=[VMEM, ANY, ANY],
        out_shape=[
            pltpu.VMEM((LAYERS, HD, D), bf16),
            jax.ShapeDtypeStruct((LAYERS, D, HD), bf16),
            pltpu.HBM((HD, D), bf16),
        ],
        scratch_shapes=[
            pltpu.VMEM((2, D, HD), bf16),
            pltpu.VMEM((HD, D), bf16),
            pltpu.VMEM((1, D, HD), bf16),
            pltpu.SemaphoreType.DMA((LAYERS,)),
            pltpu.SemaphoreType.DMA((1,)),
            pltpu.SemaphoreType.DMA((2,)),
            pltpu.SemaphoreType.DMA((1,)),
        ],
        compiler_params=pltpu.CompilerParams(vmem_limit_bytes=10 * 2**20),
        cost_estimate=COST,
        name="team_load",
    )(place, *map(in_hbm, pieces_out), *map(in_hbm, pieces_in), after)


def run_early(tick, place, x, pieces_in, pieces_out, stash, small):
    older = [] if stash is None else [stash, small]
    return pl.pallas_call(
        functools.partial(early_kernel, tick),
        in_specs=[SMEM, VMEM] + [ANY] * (16 + len(older)),
        out_specs=[VMEM, ANY, ANY],
        out_shape=[SENT, STASH, SMALL],
        input_output_aliases={18: 1, 19: 2} if older else {},
        scratch_shapes=FORWARD
        + [
            pltpu.VMEM((SLOTS, D, HD), bf16),
            pltpu.VMEM((SLOTS, HD, D), bf16),
            pltpu.SemaphoreType.DMA((SLOTS,)),
            pltpu.SemaphoreType.DMA((SLOTS,)),
        ],
        compiler_params=PARAMS,
        cost_estimate=COST,
        name="team_early",
    )(place, x, *map(in_hbm, pieces_in), *map(in_hbm, pieces_out), *map(in_hbm, older))


def run_forward(tick, place, x, held_out, pieces_in, stash, small):
    return pl.pallas_call(
        functools.partial(forward_kernel, tick),
        in_specs=[SMEM, VMEM, VMEM] + [ANY] * 10,
        out_specs=[VMEM, ANY, ANY],
        out_shape=[SENT, STASH, SMALL],
        input_output_aliases={11: 1, 12: 2},
        scratch_shapes=FORWARD + STREAM_IN,
        compiler_params=pltpu.CompilerParams(vmem_limit_bytes=14 * 2**20),
        cost_estimate=COST,
        name="team_forward",
    )(place, x, in_vmem(held_out), *map(in_hbm, pieces_in), in_hbm(stash), in_hbm(small))


def run_backward(tick, place, c, turned_out, turned_in, pieces_in, stash, small, cots):
    older = [] if cots is None else [cots]
    return pl.pallas_call(
        functools.partial(backward_kernel, tick),
        in_specs=[SMEM, VMEM, VMEM] + [ANY] * (11 + len(older)),
        out_specs=[VMEM, ANY],
        out_shape=[SENT, STASH],
        input_output_aliases={14: 1} if older else {},
        scratch_shapes=STATE
        + [
            pltpu.VMEM(STASH.shape, bf16),
            pltpu.VMEM(STASH.shape, bf16),
            pltpu.VMEM(SMALL.shape, f32),
            pltpu.SemaphoreType.DMA((LAYERS + 1,)),
            pltpu.SemaphoreType.DMA((LAYERS,)),
        ]
        + STREAM_IN
        + [pltpu.SemaphoreType.DMA((1,)), pltpu.VMEM((HD, D), bf16), pltpu.VMEM((HD, D), bf16)],
        compiler_params=PARAMS,
        cost_estimate=COST,
        name="team_backward",
    )(place, c, in_vmem(turned_out), *map(in_hbm, [turned_in, *pieces_in, stash, small, *older]))


def along_z(value, steps):
    index = [(z % 4) * 2 + z // 4 for z in range(8)]
    pairs = [(index[z], index[(z + steps) % 8]) for z in range(8)]
    return lax.ppermute(value, ("zl", "zh"), pairs)


def swap_cores(value):
    return lax.ppermute(value, "core", [(0, 1), (1, 0)])


def along_y(value, source, target):
    return lax.ppermute(value, "y", [(source, target)])


PLANE = ("zl", "core", "x", "zh")


def exchange(stash):
    flat = stash.reshape(LAYERS * PARTS, ROWS, WIDE)
    flat = lax.all_to_all(flat, PLANE, 0, 0, tiled=True)
    return flat.reshape(LAYERS * PARTS * ROWS, WIDE)


def local(inputs, gain, w_in, w_out):
    axes = ("y", "zl", "core")
    place = jnp.stack([lax.axis_index(axis) for axis in axes]).astype(jnp.int32)
    own_in, own_out = w_in[0], w_out[0]
    own_in = (own_in.astype(f32) * gain[0][:, None]).astype(bf16)
    before_in, after_out = along_z(own_in, 1), along_z(own_out, -1)
    before_out, after_in = along_z(own_out, 1), along_z(own_in, -1)
    near_in, near_out, inputs = lax.optimization_barrier((before_in, after_out, inputs))
    far_in, far_out = along_z(near_in, 1), along_z(near_out, -1)
    x = jnp.broadcast_to(inputs, (8,) + inputs.shape).reshape(64, ROWS, HD)
    x = lax.all_to_all(x, ("y", "zl", "core"), 0, 0, tiled=True)
    x = x.transpose(1, 0, 2).reshape(ROWS, D)
    (before_out, after_in, x) = lax.optimization_barrier((before_out, after_in, x))
    far_in, far_out = lax.optimization_barrier((far_in, far_out))
    pieces_in = [own_in, swap_cores(own_in), after_in, swap_cores(after_in)]
    pieces_in += [far_in, swap_cores(far_in), near_in, swap_cores(near_in)]
    pieces_out = [own_out, swap_cores(own_out), near_out, swap_cores(near_out)]
    pieces_out += [far_out, swap_cores(far_out), before_out, swap_cores(before_out)]

    stash = small = cots = None
    for tick in range(8):
        if tick > 0:
            last, x = x, along_y(x, tick - 1, tick)
        if tick < EARLY:
            x, stash, small = run_early(tick, place, x, pieces_in, pieces_out, stash, small)
            continue
        if tick == EARLY:
            held_out, turned_out, turned_in = run_load(place, pieces_in, pieces_out, last)
        x, stash, small = run_forward(tick, place, x, held_out, pieces_in, stash, small)
    x, stash_sent = lax.optimization_barrier((x, stash))
    first = exchange(stash_sent)
    for tick in range(LAST, -1, -1):
        if tick < LAST:
            x = along_y(x, tick + 1, tick)
        x, cots = run_backward(
            tick, place, x, turned_out, turned_in, pieces_in, stash, small, cots
        )

    second = exchange(cots)
    part = lax.axis_index("x") * 2 + lax.axis_index("zh")
    own_gain = lax.dynamic_slice(gain, (0, part * SLICE), (1, SLICE)).reshape(SLICE, 1)
    scale = 1.0 / math.sqrt(LAYERS * PARTS * ROWS)
    rows = (((0,), (0,)), ((), ()))
    sum_in = lax.dot_general(
        first[:, :SLICE], second[:, SLICE:], rows, preferred_element_type=f32
    )
    sum_out = lax.dot_general(
        first[:, SLICE:], second[:, :SLICE], rows, preferred_element_type=f32
    )
    grad_in = (sum_in * own_gain * scale).astype(bf16)[None]
    grad_out = (sum_out * scale).astype(bf16)[None]
    return (grad_in, grad_out)


def solution(mesh):
    axes = ("y", "zl", "core", "x", "zh")
    split = Mesh(mesh.devices.reshape(8, 4, 2, 4, 2), axes)
    section, replica = ("y", "zl", "core"), ("x", "zh")
    return jax.shard_map(
        local,
        mesh=split,
        in_specs=(
            P(None, replica, section),
            P(section, None),
            P(section, None, None),
            P(section, None, None),
        ),
        out_specs=(P(section, replica, None), P(section, None, replica)),
        check_vma=False,
    )
```

```python
import functools
import math

import jax
import jax.numpy as jnp
from jax import lax
from jax.experimental import pallas as pl
from jax.experimental.pallas import tpu as pltpu
from jax.sharding import Mesh, PartitionSpec as P

epsilon = 1e-05
f32 = jnp.float32
bf16 = jnp.bfloat16

D = 8192
HD = 128
LAYERS = 8
ROWS = 16
PARTS = 8
SLICE = D // PARTS
WIDE = SLICE + HD
LAST = 7
SLOTS = 4
AHEAD = 3
EARLY = 1


def fetch(place, pieces, held, sems, layer):
    layer = jnp.int32(layer)
    slot = lax.rem(layer, held.shape[0])
    apart = lax.rem(layer // 2 - place[1] + 4, 4)
    other = (lax.rem(layer, 2) != place[2]).astype(jnp.int32)
    which = apart * 2 + other
    for index in range(8):

        @pl.when(which == index)
        def _():
            pltpu.make_async_copy(pieces[index], held.at[slot], sems.at[slot]).start()


def await_fetch(pieces, held, sems, layer):
    slot = lax.rem(jnp.int32(layer), held.shape[0])
    pltpu.make_async_copy(pieces[0], held.at[slot], sems.at[slot]).wait()
    return slot


def forward_pass(refs, fetches, get_in, get_out):
    x_ref, sent_ref, stash_ref, small_ref = refs[:4]
    hidden, narrow, wide, small, out_sems = refs[4:]
    for layer in range(AHEAD):
        fetches(layer)
    hidden[...] = x_ref[...].astype(f32)

    def step(layer, carry):
        @pl.when(layer + AHEAD < LAYERS)
        def _():
            fetches(layer + AHEAD)

        weights = get_in(layer)
        squares = jnp.zeros((ROWS, 128), f32)
        for part in range(PARTS):
            lanes = slice(part * SLICE, (part + 1) * SLICE)
            value = hidden[:, lanes]
            wide[layer, part, :, :SLICE] = value.astype(bf16)
            narrow[:, lanes] = value.astype(bf16)
            square = value * value
            for at in range(0, SLICE, 128):
                squares = squares + square[:, at : at + 128]
        inverse = lax.rsqrt(jnp.sum(squares, axis=-1, keepdims=True) * (1.0 / D) + epsilon)
        project = inverse * jnp.dot(narrow[...], weights[...], preferred_element_type=f32)
        active = (project * jax.nn.sigmoid(project)).astype(bf16)
        small[layer, 0] = project
        small[layer, 1] = jnp.broadcast_to(inverse, (ROWS, HD))
        for part in range(PARTS):
            wide[layer, part, :, SLICE:] = active
        pltpu.make_async_copy(wide.at[layer], stash_ref.at[layer], out_sems.at[layer]).start()
        weights = get_out(layer)
        for at in range(0, D, 512):
            hidden[:, at : at + 512] += jnp.dot(
                active, weights[:, at : at + 512], preferred_element_type=f32
            )
        return carry

    lax.fori_loop(0, LAYERS, step, 0)
    last = pltpu.make_async_copy(small, small_ref, out_sems.at[LAYERS])
    last.start()
    sent_ref[...] = hidden[...].astype(bf16)
    for layer in range(LAYERS):
        pltpu.make_async_copy(wide.at[layer], stash_ref.at[layer], out_sems.at[layer]).wait()
    last.wait()


def early_kernel(tick, place, x_ref, *refs):
    pieces_in, pieces_out = refs[:8], refs[8:16]
    refs = refs[16:] if tick == 0 else refs[18:]
    state, (held_in, held_out, in_sems, held_sems) = refs[3:8], refs[8:]

    @pl.when(place[0] == tick)
    def _():
        def fetches(layer):
            fetch(place, pieces_in, held_in, in_sems, layer)
            fetch(place, pieces_out, held_out, held_sems, layer)

        forward_pass(
            (x_ref,) + tuple(refs[:3]) + tuple(state),
            fetches,
            lambda layer: held_in.at[await_fetch(pieces_in, held_in, in_sems, layer)],
            lambda layer: held_out.at[await_fetch(pieces_out, held_out, held_sems, layer)],
        )


def forward_kernel(tick, place, x_ref, held_out, *refs):
    pieces_in, refs = refs[:8], refs[10:]
    state, (held_in, in_sems) = refs[3:8], refs[8:]

    @pl.when(place[0] == tick)
    def _():
        forward_pass(
            (x_ref,) + tuple(refs[:3]) + tuple(state),
            lambda layer: fetch(place, pieces_in, held_in, in_sems, layer),
            lambda layer: held_in.at[await_fetch(pieces_in, held_in, in_sems, layer)],
            lambda layer: held_out.at[layer],
        )


def turn_kernel(keep, place, *refs):
    pieces, refs = refs[:8], refs[9:]
    turned, held, turn, sems, out_sems = (refs[1], refs[0], *refs[2:]) if keep else refs

    def begin(layer, carry):
        fetch(place, pieces, held, sems, layer)
        return carry

    lax.fori_loop(0, LAYERS, begin, 0)

    def step(layer, carry):
        slot = lax.rem(layer, 2)
        copy = pltpu.make_async_copy(turn.at[slot], turned.at[layer], out_sems.at[slot])

        @pl.when(layer >= 2)
        def _():
            copy.wait()

        await_fetch(pieces, held, sems, layer)
        for at in range(0, D, HD):
            block = slice(at, at + HD)
            if keep:
                turn[slot, block, :] = held[layer, :, block].T
            else:
                turn[slot, :, block] = held[layer, block, :].T
        copy.start()
        return carry

    lax.fori_loop(0, LAYERS, step, 0)
    for layer in range(LAYERS - 2, LAYERS):
        pltpu.make_async_copy(
            turn.at[layer % 2], turned.at[layer], out_sems.at[layer % 2]
        ).wait()


def backward_layer(layer, refs, first, second):
    (stash_ref, stash_out, cotangent, rounded, stash, wide, small, in_sems, out_sems) = refs
    for part in range(PARTS):
        lanes = slice(part * SLICE, (part + 1) * SLICE)
        value = cotangent[:, lanes].astype(bf16)
        rounded[:, lanes] = value
        wide[layer, part, :, :SLICE] = value
    upper = jnp.dot(rounded[...], first(), preferred_element_type=f32)
    project = small[layer, 0]
    inverse = small[layer, 1]
    sigma = jax.nn.sigmoid(project)
    slope = upper * sigma * (1.0 + project * (1.0 - sigma))
    factor = (slope * inverse).astype(bf16)
    for part in range(PARTS):
        wide[layer, part, :, SLICE:] = factor
    inner = jnp.sum(slope * project, axis=-1, keepdims=True) * (1.0 / D)
    inner = inner * inverse[:, :1] * inverse[:, :1]
    for part in range(PARTS):
        for at in range(0, SLICE, 512):
            lanes = slice(part * SLICE + at, part * SLICE + at + 512)
            grad = jnp.dot(factor, second(lanes), preferred_element_type=f32)
            hidden = stash[layer, part, :, at : at + 512].astype(f32)
            cotangent[:, lanes] += grad - hidden * inner
    pltpu.make_async_copy(wide.at[layer], stash_out.at[layer], out_sems.at[layer]).start()


def backward_kernel(tick, place, c_ref, turned_out, turned_in, *refs):
    stash_ref, small_in = refs[:2]
    refs = refs[2:] if tick == LAST else refs[3:]
    sent_ref, stash_out = refs[:2]
    (cotangent, rounded, stash, wide, small, in_sems, out_sems, second, sems) = refs[2:]
    common = (
        stash_ref, stash_out, cotangent, rounded, stash, wide, small, in_sems, out_sems,
    )

    def fetch_turned(layer):
        slot = lax.rem(layer, SLOTS)
        return pltpu.make_async_copy(turned_in.at[layer], second.at[slot], sems.at[slot])

    @pl.when(place[0] == tick)
    def _():
        start = pltpu.make_async_copy(small_in, small, in_sems.at[LAYERS])
        start.start()

        def begin(back, carry):
            layer = LAYERS - 1 - back
            pltpu.make_async_copy(stash_ref.at[layer], stash.at[layer], in_sems.at[layer]).start()

            @pl.when(back < AHEAD)
            def _():
                fetch_turned(layer).start()

            return carry

        lax.fori_loop(0, LAYERS, begin, 0)
        cotangent[...] = c_ref[...].astype(f32)
        start.wait()

        def step(back, carry):
            layer = LAYERS - 1 - back
            slot = lax.rem(layer, SLOTS)

            @pl.when(layer >= AHEAD)
            def _():
                fetch_turned(layer - AHEAD).start()

            fetch_turned(layer).wait()
            pltpu.make_async_copy(stash_ref.at[layer], stash.at[layer], in_sems.at[layer]).wait()
            backward_layer(
                layer, common, lambda: turned_out[layer], lambda lanes: second[slot, :, lanes]
            )
            return carry

        lax.fori_loop(0, LAYERS, step, 0)
        sent_ref[...] = cotangent[...].astype(bf16)

        def end(layer, carry):
            pltpu.make_async_copy(wide.at[layer], stash_out.at[layer], out_sems.at[layer]).wait()
            return carry

        lax.fori_loop(0, LAYERS, end, 0)


STASH = pltpu.HBM((LAYERS, PARTS, ROWS, WIDE), bf16)
SMALL = pltpu.HBM((LAYERS, 2, ROWS, HD), f32)
SENT = jax.ShapeDtypeStruct((ROWS, D), bf16)
ANY = pl.BlockSpec(memory_space=pl.ANY)
VMEM = pl.BlockSpec(memory_space=pltpu.VMEM)
SMEM = pl.BlockSpec(memory_space=pltpu.SMEM)
STATE = [pltpu.VMEM((ROWS, D), f32), pltpu.VMEM((ROWS, D), bf16)]
PARAMS = pltpu.CompilerParams(vmem_limit_bytes=20 * 2**20)


COST = pl.CostEstimate(flops=4 * LAYERS * ROWS * D * HD, bytes_accessed=36 * 2**20, transcendentals=0)


def in_hbm(value):
    return pltpu.with_memory_space_constraint(value, pltpu.HBM)


def in_vmem(value):
    return pltpu.with_memory_space_constraint(value, pltpu.VMEM)


STREAM_IN = [pltpu.VMEM((SLOTS, D, HD), bf16), pltpu.SemaphoreType.DMA((SLOTS,))]
FORWARD = STATE + [
    pltpu.VMEM(STASH.shape, bf16),
    pltpu.VMEM(SMALL.shape, f32),
    pltpu.SemaphoreType.DMA((LAYERS + 1,)),
]


def run_turn(keep, place, pieces, after):
    tall, flat = (LAYERS, D, HD), (LAYERS, HD, D)
    turned = tall if keep else flat
    held = pltpu.VMEM(flat if keep else tall, bf16)
    return pl.pallas_call(
        functools.partial(turn_kernel, keep),
        in_specs=[SMEM] + [ANY] * 9,
        out_specs=[VMEM, ANY] if keep else ANY,
        out_shape=[held, pltpu.HBM(turned, bf16)] if keep else pltpu.HBM(turned, bf16),
        scratch_shapes=([] if keep else [held])
        + [
            pltpu.VMEM((2,) + turned[1:], bf16),
            pltpu.SemaphoreType.DMA((LAYERS,)),
            pltpu.SemaphoreType.DMA((2,)),
        ],
        compiler_params=pltpu.CompilerParams(vmem_limit_bytes=(6 if keep else 22) * 2**20),
        cost_estimate=COST,
        name="team_turn",
    )(place, *map(in_hbm, pieces), after)


def run_early(tick, place, x, pieces_in, pieces_out, stash, small):
    older = [] if stash is None else [stash, small]
    return pl.pallas_call(
        functools.partial(early_kernel, tick),
        in_specs=[SMEM, VMEM] + [ANY] * (16 + len(older)),
        out_specs=[VMEM, ANY, ANY],
        out_shape=[SENT, STASH, SMALL],
        input_output_aliases={18: 1, 19: 2} if older else {},
        scratch_shapes=FORWARD
        + [
            pltpu.VMEM((SLOTS, D, HD), bf16),
            pltpu.VMEM((SLOTS, HD, D), bf16),
            pltpu.SemaphoreType.DMA((SLOTS,)),
            pltpu.SemaphoreType.DMA((SLOTS,)),
        ],
        compiler_params=PARAMS,
        cost_estimate=COST,
        name="team_early",
    )(place, x, *map(in_hbm, pieces_in), *map(in_hbm, pieces_out), *map(in_hbm, older))


def run_forward(tick, place, x, held_out, pieces_in, stash, small):
    return pl.pallas_call(
        functools.partial(forward_kernel, tick),
        in_specs=[SMEM, VMEM, VMEM] + [ANY] * 10,
        out_specs=[VMEM, ANY, ANY],
        out_shape=[SENT, STASH, SMALL],
        input_output_aliases={11: 1, 12: 2},
        scratch_shapes=FORWARD + STREAM_IN,
        compiler_params=pltpu.CompilerParams(vmem_limit_bytes=14 * 2**20),
        cost_estimate=COST,
        name="team_forward",
    )(place, x, in_vmem(held_out), *map(in_hbm, pieces_in), in_hbm(stash), in_hbm(small))


def run_backward(tick, place, c, turned_out, turned_in, stash, small, cots):
    older = [] if cots is None else [cots]
    return pl.pallas_call(
        functools.partial(backward_kernel, tick),
        in_specs=[SMEM, VMEM, VMEM] + [ANY] * (3 + len(older)),
        out_specs=[VMEM, ANY],
        out_shape=[SENT, STASH],
        input_output_aliases={6: 1} if older else {},
        scratch_shapes=STATE
        + [
            pltpu.VMEM(STASH.shape, bf16),
            pltpu.VMEM(STASH.shape, bf16),
            pltpu.VMEM(SMALL.shape, f32),
            pltpu.SemaphoreType.DMA((LAYERS + 1,)),
            pltpu.SemaphoreType.DMA((LAYERS,)),
            pltpu.VMEM((SLOTS, HD, D), bf16),
            pltpu.SemaphoreType.DMA((SLOTS,)),
        ],
        compiler_params=pltpu.CompilerParams(vmem_limit_bytes=16 * 2**20),
        cost_estimate=COST,
        name="team_backward",
    )(place, c, in_vmem(turned_out), *map(in_hbm, [turned_in, stash, small, *older]))


def along_z(value, steps):
    index = [(z % 4) * 2 + z // 4 for z in range(8)]
    pairs = [(index[z], index[(z + steps) % 8]) for z in range(8)]
    return lax.ppermute(value, ("zl", "zh"), pairs)


def swap_cores(value):
    return lax.ppermute(value, "core", [(0, 1), (1, 0)])


def along_y(value, source, target):
    return lax.ppermute(value, "y", [(source, target)])


PLANE = ("zl", "core", "x", "zh")


def exchange(stash):
    flat = stash.reshape(LAYERS * PARTS, ROWS, WIDE)
    flat = lax.all_to_all(flat, PLANE, 0, 0, tiled=True)
    return flat.reshape(LAYERS * PARTS * ROWS, WIDE)


def local(inputs, gain, w_in, w_out):
    axes = ("y", "zl", "core")
    place = jnp.stack([lax.axis_index(axis) for axis in axes]).astype(jnp.int32)
    own_in, own_out = w_in[0], w_out[0]
    own_in = (own_in.astype(f32) * gain[0][:, None]).astype(bf16)
    before_in, after_out = along_z(own_in, 1), along_z(own_out, -1)
    before_out, after_in = along_z(own_out, 1), along_z(own_in, -1)
    near_in, near_out, inputs = lax.optimization_barrier((before_in, after_out, inputs))
    far_in, far_out = along_z(near_in, 1), along_z(near_out, -1)
    x = jnp.broadcast_to(inputs, (8,) + inputs.shape).reshape(64, ROWS, HD)
    x = lax.all_to_all(x, ("y", "zl", "core"), 0, 0, tiled=True)
    x = x.transpose(1, 0, 2).reshape(ROWS, D)
    (before_out, after_in, x) = lax.optimization_barrier((before_out, after_in, x))
    far_in, far_out = lax.optimization_barrier((far_in, far_out))
    pieces_in = [own_in, swap_cores(own_in), after_in, swap_cores(after_in)]
    pieces_in += [far_in, swap_cores(far_in), near_in, swap_cores(near_in)]
    pieces_out = [own_out, swap_cores(own_out), near_out, swap_cores(near_out)]
    pieces_out += [far_out, swap_cores(far_out), before_out, swap_cores(before_out)]

    stash = small = cots = None
    for tick in range(8):
        if tick > 0:
            last, x = x, along_y(x, tick - 1, tick)
        if tick < EARLY:
            x, stash, small = run_early(tick, place, x, pieces_in, pieces_out, stash, small)
            continue
        if tick == EARLY:
            held_out, turned_out = run_turn(True, place, pieces_out, last)
        if tick == EARLY + 1:
            turned_in = run_turn(False, place, pieces_in, last)
            x, turned_in = lax.optimization_barrier((x, turned_in))
        x, stash, small = run_forward(tick, place, x, held_out, pieces_in, stash, small)
    x, stash_sent = lax.optimization_barrier((x, stash))
    first = exchange(stash_sent)
    for tick in range(LAST, -1, -1):
        if tick < LAST:
            x = along_y(x, tick + 1, tick)
        x, cots = run_backward(tick, place, x, turned_out, turned_in, stash, small, cots)

    second = exchange(cots)
    part = lax.axis_index("x") * 2 + lax.axis_index("zh")
    own_gain = lax.dynamic_slice(gain, (0, part * SLICE), (1, SLICE)).reshape(SLICE, 1)
    scale = 1.0 / math.sqrt(LAYERS * PARTS * ROWS)
    rows = (((0,), (0,)), ((), ()))
    sum_in = lax.dot_general(
        first[:, :SLICE], second[:, SLICE:], rows, preferred_element_type=f32
    )
    sum_out = lax.dot_general(
        first[:, SLICE:], second[:, :SLICE], rows, preferred_element_type=f32
    )
    grad_in = (sum_in * own_gain * scale).astype(bf16)[None]
    grad_out = (sum_out * scale).astype(bf16)[None]
    return (grad_in, grad_out)


def solution(mesh):
    axes = ("y", "zl", "core", "x", "zh")
    split = Mesh(mesh.devices.reshape(8, 4, 2, 4, 2), axes)
    section, replica = ("y", "zl", "core"), ("x", "zh")
    return jax.shard_map(
        local,
        mesh=split,
        in_specs=(
            P(None, replica, section),
            P(section, None),
            P(section, None, None),
            P(section, None, None),
        ),
        out_specs=(P(section, replica, None), P(section, None, replica)),
        check_vma=False,
    )
```

```python
import functools
import math

import jax
import jax.numpy as jnp
from jax import lax
from jax.experimental import pallas as pl
from jax.experimental.pallas import tpu as pltpu
from jax.sharding import Mesh, PartitionSpec as P

epsilon = 1e-05
f32 = jnp.float32
bf16 = jnp.bfloat16

D = 8192
HD = 128
LAYERS = 8
ROWS = 16
PARTS = 8
SLICE = D // PARTS
WIDE = SLICE + HD
LAST = 7
SLOTS = 4
AHEAD = 3
EARLY = 1


def fetch(place, pieces, held, sems, layer):
    layer = jnp.int32(layer)
    slot = lax.rem(layer, held.shape[0])
    apart = lax.rem(layer // 2 - place[1] + 4, 4)
    other = (lax.rem(layer, 2) != place[2]).astype(jnp.int32)
    which = apart * 2 + other
    for index in range(8):

        @pl.when(which == index)
        def _():
            pltpu.make_async_copy(pieces[index], held.at[slot], sems.at[slot]).start()


def await_fetch(pieces, held, sems, layer):
    slot = lax.rem(jnp.int32(layer), held.shape[0])
    pltpu.make_async_copy(pieces[0], held.at[slot], sems.at[slot]).wait()
    return slot


def forward_pass(refs, fetches, get_in, get_out):
    x_ref, sent_ref, stash_ref, small_ref = refs[:4]
    hidden, narrow, wide, small, out_sems = refs[4:]
    for layer in range(AHEAD if fetches else 0):
        fetches(layer)
    hidden[...] = x_ref[...].astype(f32)

    def step(layer, carry):
        if fetches:

            @pl.when(layer + AHEAD < LAYERS)
            def _():
                fetches(layer + AHEAD)

        weights = get_in(layer)
        squares = jnp.zeros((ROWS, 128), f32)
        for part in range(PARTS):
            lanes = slice(part * SLICE, (part + 1) * SLICE)
            value = hidden[:, lanes]
            wide[layer, part, :, :SLICE] = value.astype(bf16)
            narrow[:, lanes] = value.astype(bf16)
            square = value * value
            for at in range(0, SLICE, 128):
                squares = squares + square[:, at : at + 128]
        inverse = lax.rsqrt(jnp.sum(squares, axis=-1, keepdims=True) * (1.0 / D) + epsilon)
        project = inverse * jnp.dot(narrow[...], weights[...], preferred_element_type=f32)
        active = (project * jax.nn.sigmoid(project)).astype(bf16)
        small[layer, 0] = project
        small[layer, 1] = jnp.broadcast_to(inverse, (ROWS, HD))
        for part in range(PARTS):
            wide[layer, part, :, SLICE:] = active
        pltpu.make_async_copy(wide.at[layer], stash_ref.at[layer], out_sems.at[layer]).start()
        weights = get_out(layer)
        for at in range(0, D, 512):
            hidden[:, at : at + 512] += jnp.dot(
                active, weights[:, at : at + 512], preferred_element_type=f32
            )
        return carry

    lax.fori_loop(0, LAYERS, step, 0)
    last = pltpu.make_async_copy(small, small_ref, out_sems.at[LAYERS])
    last.start()
    sent_ref[...] = hidden[...].astype(bf16)
    for layer in range(LAYERS):
        pltpu.make_async_copy(wide.at[layer], stash_ref.at[layer], out_sems.at[layer]).wait()
    last.wait()


def early_kernel(tick, place, x_ref, *refs):
    pieces_in, pieces_out = refs[:8], refs[8:16]
    refs = refs[16:] if tick == 0 else refs[18:]
    state, (held_in, held_out, in_sems, held_sems) = refs[3:8], refs[8:]

    @pl.when(place[0] == tick)
    def _():
        def fetches(layer):
            fetch(place, pieces_in, held_in, in_sems, layer)
            fetch(place, pieces_out, held_out, held_sems, layer)

        forward_pass(
            (x_ref,) + tuple(refs[:3]) + tuple(state),
            fetches,
            lambda layer: held_in.at[await_fetch(pieces_in, held_in, in_sems, layer)],
            lambda layer: held_out.at[await_fetch(pieces_out, held_out, held_sems, layer)],
        )


def forward_kernel(tick, place, x_ref, held_out, *refs):
    if tick == EARLY:
        pieces_in, refs = refs[:8], refs[10:]
        state, (held_in, in_sems) = refs[3:8], refs[8:]
    else:
        held_in, refs = refs[0], refs[3:]
        state = refs[3:8]

    @pl.when(place[0] == tick)
    def _():
        if tick == EARLY:
            fetches = lambda layer: fetch(place, pieces_in, held_in, in_sems, layer)
            get_in = lambda layer: held_in.at[await_fetch(pieces_in, held_in, in_sems, layer)]
        else:
            fetches, get_in = None, lambda layer: held_in.at[layer]
        forward_pass(
            (x_ref,) + tuple(refs[:3]) + tuple(state),
            fetches,
            get_in,
            lambda layer: held_out.at[layer],
        )


def turn_kernel(tall, place, *refs):
    pieces, refs = refs[:8], refs[9:]
    held, turned, turn, sems, out_sems = refs

    def begin(layer, carry):
        fetch(place, pieces, held, sems, layer)
        return carry

    lax.fori_loop(0, LAYERS, begin, 0)

    def step(layer, carry):
        slot = lax.rem(layer, 2)
        copy = pltpu.make_async_copy(turn.at[slot], turned.at[layer], out_sems.at[slot])

        @pl.when(layer >= 2)
        def _():
            copy.wait()

        await_fetch(pieces, held, sems, layer)
        for at in range(0, D, HD):
            block = slice(at, at + HD)
            if tall:
                turn[slot, :, block] = held[layer, block, :].T
            else:
                turn[slot, block, :] = held[layer, :, block].T
        copy.start()
        return carry

    lax.fori_loop(0, LAYERS, step, 0)
    for layer in range(LAYERS - 2, LAYERS):
        pltpu.make_async_copy(
            turn.at[layer % 2], turned.at[layer], out_sems.at[layer % 2]
        ).wait()


def backward_layer(layer, refs, first, second):
    (stash_ref, stash_out, cotangent, rounded, stash, wide, small, in_sems, out_sems) = refs
    for part in range(PARTS):
        lanes = slice(part * SLICE, (part + 1) * SLICE)
        value = cotangent[:, lanes].astype(bf16)
        rounded[:, lanes] = value
        wide[layer, part, :, :SLICE] = value
    upper = jnp.dot(rounded[...], first(), preferred_element_type=f32)
    project = small[layer, 0]
    inverse = small[layer, 1]
    sigma = jax.nn.sigmoid(project)
    slope = upper * sigma * (1.0 + project * (1.0 - sigma))
    factor = (slope * inverse).astype(bf16)
    for part in range(PARTS):
        wide[layer, part, :, SLICE:] = factor
    inner = jnp.sum(slope * project, axis=-1, keepdims=True) * (1.0 / D)
    inner = inner * inverse[:, :1] * inverse[:, :1]
    for part in range(PARTS):
        for at in range(0, SLICE, 512):
            lanes = slice(part * SLICE + at, part * SLICE + at + 512)
            grad = jnp.dot(factor, second(lanes), preferred_element_type=f32)
            hidden = stash[layer, part, :, at : at + 512].astype(f32)
            cotangent[:, lanes] += grad - hidden * inner
    pltpu.make_async_copy(wide.at[layer], stash_out.at[layer], out_sems.at[layer]).start()


def backward_kernel(tick, place, c_ref, turned_out, turned_in, *refs):
    stash_ref, small_in = refs[:2]
    refs = refs[2:] if tick == LAST else refs[3:]
    sent_ref, stash_out = refs[:2]
    (cotangent, rounded, stash, wide, small, in_sems, out_sems, second, sems) = refs[2:]
    common = (
        stash_ref, stash_out, cotangent, rounded, stash, wide, small, in_sems, out_sems,
    )

    def fetch_turned(layer):
        slot = lax.rem(layer, SLOTS)
        return pltpu.make_async_copy(turned_in.at[layer], second.at[slot], sems.at[slot])

    @pl.when(place[0] == tick)
    def _():
        start = pltpu.make_async_copy(small_in, small, in_sems.at[LAYERS])
        start.start()

        def begin(back, carry):
            layer = LAYERS - 1 - back
            pltpu.make_async_copy(stash_ref.at[layer], stash.at[layer], in_sems.at[layer]).start()

            @pl.when(back < AHEAD)
            def _():
                fetch_turned(layer).start()

            return carry

        lax.fori_loop(0, LAYERS, begin, 0)
        cotangent[...] = c_ref[...].astype(f32)
        start.wait()

        def step(back, carry):
            layer = LAYERS - 1 - back
            slot = lax.rem(layer, SLOTS)

            @pl.when(layer >= AHEAD)
            def _():
                fetch_turned(layer - AHEAD).start()

            fetch_turned(layer).wait()
            pltpu.make_async_copy(stash_ref.at[layer], stash.at[layer], in_sems.at[layer]).wait()
            backward_layer(
                layer, common, lambda: turned_out[layer], lambda lanes: second[slot, :, lanes]
            )
            return carry

        lax.fori_loop(0, LAYERS, step, 0)
        sent_ref[...] = cotangent[...].astype(bf16)

        def end(layer, carry):
            pltpu.make_async_copy(wide.at[layer], stash_out.at[layer], out_sems.at[layer]).wait()
            return carry

        lax.fori_loop(0, LAYERS, end, 0)


STASH = pltpu.HBM((LAYERS, PARTS, ROWS, WIDE), bf16)
SMALL = pltpu.HBM((LAYERS, 2, ROWS, HD), f32)
SENT = jax.ShapeDtypeStruct((ROWS, D), bf16)
ANY = pl.BlockSpec(memory_space=pl.ANY)
VMEM = pl.BlockSpec(memory_space=pltpu.VMEM)
SMEM = pl.BlockSpec(memory_space=pltpu.SMEM)
STATE = [pltpu.VMEM((ROWS, D), f32), pltpu.VMEM((ROWS, D), bf16)]
PARAMS = pltpu.CompilerParams(vmem_limit_bytes=20 * 2**20)


COST = pl.CostEstimate(flops=4 * LAYERS * ROWS * D * HD, bytes_accessed=36 * 2**20, transcendentals=0)


def in_hbm(value):
    return pltpu.with_memory_space_constraint(value, pltpu.HBM)


def in_vmem(value):
    return pltpu.with_memory_space_constraint(value, pltpu.VMEM)


STREAM_IN = [pltpu.VMEM((SLOTS, D, HD), bf16), pltpu.SemaphoreType.DMA((SLOTS,))]
FORWARD = STATE + [
    pltpu.VMEM(STASH.shape, bf16),
    pltpu.VMEM(SMALL.shape, f32),
    pltpu.SemaphoreType.DMA((LAYERS + 1,)),
]


def run_turn(place, pieces, after):
    rows, columns = pieces[0].shape
    return pl.pallas_call(
        functools.partial(turn_kernel, rows > columns),
        in_specs=[SMEM] + [ANY] * 9,
        out_specs=[VMEM, ANY],
        out_shape=[
            pltpu.VMEM((LAYERS, rows, columns), bf16),
            pltpu.HBM((LAYERS, columns, rows), bf16),
        ],
        scratch_shapes=[
            pltpu.VMEM((2, columns, rows), bf16),
            pltpu.SemaphoreType.DMA((LAYERS,)),
            pltpu.SemaphoreType.DMA((2,)),
        ],
        compiler_params=pltpu.CompilerParams(vmem_limit_bytes=6 * 2**20),
        cost_estimate=COST,
        name="team_turn",
    )(place, *map(in_hbm, pieces), after)


def run_early(tick, place, x, pieces_in, pieces_out, stash, small):
    older = [] if stash is None else [stash, small]
    return pl.pallas_call(
        functools.partial(early_kernel, tick),
        in_specs=[SMEM, VMEM] + [ANY] * (16 + len(older)),
        out_specs=[VMEM, ANY, ANY],
        out_shape=[SENT, STASH, SMALL],
        input_output_aliases={18: 1, 19: 2} if older else {},
        scratch_shapes=FORWARD
        + [
            pltpu.VMEM((SLOTS, D, HD), bf16),
            pltpu.VMEM((SLOTS, HD, D), bf16),
            pltpu.SemaphoreType.DMA((SLOTS,)),
            pltpu.SemaphoreType.DMA((SLOTS,)),
        ],
        compiler_params=PARAMS,
        cost_estimate=COST,
        name="team_early",
    )(place, x, *map(in_hbm, pieces_in), *map(in_hbm, pieces_out), *map(in_hbm, older))


def run_forward(tick, place, x, held_out, weights_in, stash, small):
    resident = tick > EARLY
    weights_in = [in_vmem(weights_in)] if resident else [*map(in_hbm, weights_in)]
    count = len(weights_in)
    return pl.pallas_call(
        functools.partial(forward_kernel, tick),
        in_specs=[SMEM, VMEM, VMEM] + [VMEM if resident else ANY] * count + [ANY] * 2,
        out_specs=[VMEM, ANY, ANY],
        out_shape=[SENT, STASH, SMALL],
        input_output_aliases={3 + count: 1, 4 + count: 2},
        scratch_shapes=FORWARD + ([] if resident else STREAM_IN),
        compiler_params=pltpu.CompilerParams(vmem_limit_bytes=(6 if resident else 14) * 2**20),
        cost_estimate=COST,
        name="team_forward",
    )(place, x, in_vmem(held_out), *weights_in, in_hbm(stash), in_hbm(small))


def run_backward(tick, place, c, turned_out, turned_in, stash, small, cots):
    older = [] if cots is None else [cots]
    return pl.pallas_call(
        functools.partial(backward_kernel, tick),
        in_specs=[SMEM, VMEM, VMEM] + [ANY] * (3 + len(older)),
        out_specs=[VMEM, ANY],
        out_shape=[SENT, STASH],
        input_output_aliases={6: 1} if older else {},
        scratch_shapes=STATE
        + [
            pltpu.VMEM(STASH.shape, bf16),
            pltpu.VMEM(STASH.shape, bf16),
            pltpu.VMEM(SMALL.shape, f32),
            pltpu.SemaphoreType.DMA((LAYERS + 1,)),
            pltpu.SemaphoreType.DMA((LAYERS,)),
            pltpu.VMEM((SLOTS, HD, D), bf16),
            pltpu.SemaphoreType.DMA((SLOTS,)),
        ],
        compiler_params=pltpu.CompilerParams(vmem_limit_bytes=16 * 2**20),
        cost_estimate=COST,
        name="team_backward",
    )(place, c, in_vmem(turned_out), *map(in_hbm, [turned_in, stash, small, *older]))


def along_z(value, steps):
    index = [(z % 4) * 2 + z // 4 for z in range(8)]
    pairs = [(index[z], index[(z + steps) % 8]) for z in range(8)]
    return lax.ppermute(value, ("zl", "zh"), pairs)


def swap_cores(value):
    return lax.ppermute(value, "core", [(0, 1), (1, 0)])


def along_y(value, source, target):
    return lax.ppermute(value, "y", [(source, target)])


PLANE = ("zl", "core", "x", "zh")


def exchange(stash):
    flat = stash.reshape(LAYERS * PARTS, ROWS, WIDE)
    flat = lax.all_to_all(flat, PLANE, 0, 0, tiled=True)
    return flat.reshape(LAYERS * PARTS * ROWS, WIDE)


def local(inputs, gain, w_in, w_out):
    axes = ("y", "zl", "core")
    place = jnp.stack([lax.axis_index(axis) for axis in axes]).astype(jnp.int32)
    own_in, own_out = w_in[0], w_out[0]
    own_in = (own_in.astype(f32) * gain[0][:, None]).astype(bf16)
    before_in, after_out = along_z(own_in, 1), along_z(own_out, -1)
    before_out, after_in = along_z(own_out, 1), along_z(own_in, -1)
    near_in, near_out, inputs = lax.optimization_barrier((before_in, after_out, inputs))
    far_in, far_out = along_z(near_in, 1), along_z(near_out, -1)
    x = jnp.broadcast_to(inputs, (8,) + inputs.shape).reshape(64, ROWS, HD)
    x = lax.all_to_all(x, ("y", "zl", "core"), 0, 0, tiled=True)
    x = x.transpose(1, 0, 2).reshape(ROWS, D)
    (before_out, after_in, x) = lax.optimization_barrier((before_out, after_in, x))
    far_in, far_out = lax.optimization_barrier((far_in, far_out))
    pieces_in = [own_in, swap_cores(own_in), after_in, swap_cores(after_in)]
    pieces_in += [far_in, swap_cores(far_in), near_in, swap_cores(near_in)]
    pieces_out = [own_out, swap_cores(own_out), near_out, swap_cores(near_out)]
    pieces_out += [far_out, swap_cores(far_out), before_out, swap_cores(before_out)]

    stash = small = cots = None
    for tick in range(8):
        if tick > 0:
            last, x = x, along_y(x, tick - 1, tick)
        if tick < EARLY:
            x, stash, small = run_early(tick, place, x, pieces_in, pieces_out, stash, small)
            continue
        if tick == EARLY:
            held_out, turned_out = run_turn(place, pieces_out, last)
            weights_in = pieces_in
        if tick == EARLY + 1:
            weights_in, turned_in = run_turn(place, pieces_in, last)
            x, turned_in = lax.optimization_barrier((x, turned_in))
        x, stash, small = run_forward(tick, place, x, held_out, weights_in, stash, small)
    x, stash_sent = lax.optimization_barrier((x, stash))
    first = exchange(stash_sent)
    for tick in range(LAST, -1, -1):
        if tick < LAST:
            x = along_y(x, tick + 1, tick)
        x, cots = run_backward(tick, place, x, turned_out, turned_in, stash, small, cots)

    second = exchange(cots)
    part = lax.axis_index("x") * 2 + lax.axis_index("zh")
    own_gain = lax.dynamic_slice(gain, (0, part * SLICE), (1, SLICE)).reshape(SLICE, 1)
    scale = 1.0 / math.sqrt(LAYERS * PARTS * ROWS)
    rows = (((0,), (0,)), ((), ()))
    sum_in = lax.dot_general(
        first[:, :SLICE], second[:, SLICE:], rows, preferred_element_type=f32
    )
    sum_out = lax.dot_general(
        first[:, SLICE:], second[:, :SLICE], rows, preferred_element_type=f32
    )
    grad_in = (sum_in * own_gain * scale).astype(bf16)[None]
    grad_out = (sum_out * scale).astype(bf16)[None]
    return (grad_in, grad_out)


def solution(mesh):
    axes = ("y", "zl", "core", "x", "zh")
    split = Mesh(mesh.devices.reshape(8, 4, 2, 4, 2), axes)
    section, replica = ("y", "zl", "core"), ("x", "zh")
    return jax.shard_map(
        local,
        mesh=split,
        in_specs=(
            P(None, replica, section),
            P(section, None),
            P(section, None, None),
            P(section, None, None),
        ),
        out_specs=(P(section, replica, None), P(section, None, replica)),
        check_vma=False,
    )
```

```python
import functools
import math

import jax
import jax.numpy as jnp
from jax import lax
from jax.experimental import pallas as pl
from jax.experimental.pallas import tpu as pltpu
from jax.sharding import Mesh, PartitionSpec as P

epsilon = 1e-05
f32 = jnp.float32
bf16 = jnp.bfloat16

D = 8192
HD = 128
LAYERS = 8
ROWS = 16
PARTS = 8
SLICE = D // PARTS
WIDE = SLICE + HD
LAST = 7
SLOTS = 4
AHEAD = 3
EARLY = 1


def fetch(place, pieces, held, sems, layer):
    layer = jnp.int32(layer)
    slot = lax.rem(layer, held.shape[0])
    apart = lax.rem(layer // 2 - place[1] + 4, 4)
    other = (lax.rem(layer, 2) != place[2]).astype(jnp.int32)
    which = apart * 2 + other
    for index in range(8):

        @pl.when(which == index)
        def _():
            pltpu.make_async_copy(pieces[index], held.at[slot], sems.at[slot]).start()


def await_fetch(pieces, held, sems, layer):
    slot = lax.rem(jnp.int32(layer), held.shape[0])
    pltpu.make_async_copy(pieces[0], held.at[slot], sems.at[slot]).wait()
    return slot


def forward_pass(refs, fetches, get_in, get_out):
    x_ref, sent_ref, stash_ref, small_ref = refs[:4]
    hidden, narrow, wide, small, out_sems = refs[4:]
    for layer in range(AHEAD if fetches else 0):
        fetches(layer)
    hidden[...] = x_ref[...].astype(f32)

    def step(layer, carry):
        if fetches:

            @pl.when(layer + AHEAD < LAYERS)
            def _():
                fetches(layer + AHEAD)

        weights = get_in(layer)
        squares = jnp.zeros((ROWS, 128), f32)
        for part in range(PARTS):
            lanes = slice(part * SLICE, (part + 1) * SLICE)
            value = hidden[:, lanes]
            wide[layer, part, :, :SLICE] = value.astype(bf16)
            narrow[:, lanes] = value.astype(bf16)
            square = value * value
            for at in range(0, SLICE, 128):
                squares = squares + square[:, at : at + 128]
        inverse = lax.rsqrt(jnp.sum(squares, axis=-1, keepdims=True) * (1.0 / D) + epsilon)
        project = inverse * jnp.dot(narrow[...], weights[...], preferred_element_type=f32)
        active = (project * jax.nn.sigmoid(project)).astype(bf16)
        small[layer, 0] = project
        small[layer, 1] = jnp.broadcast_to(inverse, (ROWS, HD))
        for part in range(PARTS):
            wide[layer, part, :, SLICE:] = active
        pltpu.make_async_copy(wide.at[layer], stash_ref.at[layer], out_sems.at[layer]).start()
        weights = get_out(layer)
        for at in range(0, D, 512):
            hidden[:, at : at + 512] += jnp.dot(
                active, weights[:, at : at + 512], preferred_element_type=f32
            )
        return carry

    lax.fori_loop(0, LAYERS, step, 0)
    last = pltpu.make_async_copy(small, small_ref, out_sems.at[LAYERS])
    last.start()
    sent_ref[...] = hidden[...].astype(bf16)
    for layer in range(LAYERS):
        pltpu.make_async_copy(wide.at[layer], stash_ref.at[layer], out_sems.at[layer]).wait()
    last.wait()


def early_kernel(tick, place, x_ref, *refs):
    pieces_in, pieces_out = refs[:8], refs[8:16]
    refs = refs[16:] if tick == 0 else refs[18:]
    state, (held_in, held_out, in_sems, held_sems) = refs[3:8], refs[8:]

    @pl.when(place[0] == tick)
    def _():
        def fetches(layer):
            fetch(place, pieces_in, held_in, in_sems, layer)
            fetch(place, pieces_out, held_out, held_sems, layer)

        forward_pass(
            (x_ref,) + tuple(refs[:3]) + tuple(state),
            fetches,
            lambda layer: held_in.at[await_fetch(pieces_in, held_in, in_sems, layer)],
            lambda layer: held_out.at[await_fetch(pieces_out, held_out, held_sems, layer)],
        )


def forward_kernel(tick, place, x_ref, held_out, *refs):
    if tick == EARLY:
        pieces_in, refs = refs[:8], refs[10:]
        state, (held_in, in_sems) = refs[3:8], refs[8:]
    else:
        held_in, refs = refs[0], refs[3:]
        state = refs[3:8]

    @pl.when(place[0] == tick)
    def _():
        if tick == EARLY:
            fetches = lambda layer: fetch(place, pieces_in, held_in, in_sems, layer)
            get_in = lambda layer: held_in.at[await_fetch(pieces_in, held_in, in_sems, layer)]
        else:
            fetches, get_in = None, lambda layer: held_in.at[layer]
        forward_pass(
            (x_ref,) + tuple(refs[:3]) + tuple(state),
            fetches,
            get_in,
            lambda layer: held_out.at[layer],
        )


def turn_kernel(tall, place, *refs):
    pieces, refs = refs[:8], refs[9:]
    held, turned, turn, sems, out_sems = refs

    def begin(layer, carry):
        fetch(place, pieces, held, sems, layer)
        return carry

    lax.fori_loop(0, LAYERS, begin, 0)

    def step(layer, carry):
        slot = lax.rem(layer, 2)
        copy = pltpu.make_async_copy(turn.at[slot], turned.at[layer], out_sems.at[slot])

        @pl.when(layer >= 2)
        def _():
            copy.wait()

        await_fetch(pieces, held, sems, layer)
        for at in range(0, D, HD):
            block = slice(at, at + HD)
            if tall:
                turn[slot, :, block] = held[layer, block, :].T
            else:
                turn[slot, block, :] = held[layer, :, block].T
        copy.start()
        return carry

    lax.fori_loop(0, LAYERS, step, 0)
    for layer in range(LAYERS - 2, LAYERS):
        pltpu.make_async_copy(
            turn.at[layer % 2], turned.at[layer], out_sems.at[layer % 2]
        ).wait()


def backward_layer(layer, refs, first, second):
    (stash_ref, stash_out, cotangent, rounded, stash, wide, small, in_sems, out_sems) = refs
    for part in range(PARTS):
        lanes = slice(part * SLICE, (part + 1) * SLICE)
        value = cotangent[:, lanes].astype(bf16)
        rounded[:, lanes] = value
        wide[layer, part, :, :SLICE] = value
    upper = jnp.dot(rounded[...], first(), preferred_element_type=f32)
    project = small[layer, 0]
    inverse = small[layer, 1]
    sigma = jax.nn.sigmoid(project)
    slope = upper * sigma * (1.0 + project * (1.0 - sigma))
    factor = (slope * inverse).astype(bf16)
    for part in range(PARTS):
        wide[layer, part, :, SLICE:] = factor
    inner = jnp.sum(slope * project, axis=-1, keepdims=True) * (1.0 / D)
    inner = inner * inverse[:, :1] * inverse[:, :1]
    for part in range(PARTS):
        for at in range(0, SLICE, 512):
            lanes = slice(part * SLICE + at, part * SLICE + at + 512)
            grad = jnp.dot(factor, second(lanes), preferred_element_type=f32)
            hidden = stash[layer, part, :, at : at + 512].astype(f32)
            cotangent[:, lanes] += grad - hidden * inner
    pltpu.make_async_copy(wide.at[layer], stash_out.at[layer], out_sems.at[layer]).start()


def backward_kernel(tick, place, c_ref, turned_out, turned_in, *refs):
    stash_ref, small_in = refs[:2]
    refs = refs[2:] if tick == LAST else refs[3:]
    sent_ref, stash_out = refs[:2]
    (cotangent, rounded, stash, wide, small, in_sems, out_sems, second, sems, *extra) = refs[2:]
    common = (
        stash_ref, stash_out, cotangent, rounded, stash, wide, small, in_sems, out_sems,
    )

    def fetch_turned(layer):
        slot = lax.rem(layer, SLOTS)
        copies = [pltpu.make_async_copy(turned_in.at[layer], second.at[slot], sems.at[slot])]
        if extra:
            first, first_sems = extra
            copies = [
                pltpu.make_async_copy(turned_out.at[layer], first.at[slot], first_sems.at[slot])
            ] + copies
        return copies

    @pl.when(place[0] == tick)
    def _():
        start = pltpu.make_async_copy(small_in, small, in_sems.at[LAYERS])
        start.start()

        def begin(back, carry):
            layer = LAYERS - 1 - back
            pltpu.make_async_copy(stash_ref.at[layer], stash.at[layer], in_sems.at[layer]).start()

            @pl.when(back < AHEAD)
            def _():
                for copy in fetch_turned(layer):
                    copy.start()

            return carry

        lax.fori_loop(0, LAYERS, begin, 0)
        cotangent[...] = c_ref[...].astype(f32)
        start.wait()

        def step(back, carry):
            layer = LAYERS - 1 - back
            slot = lax.rem(layer, SLOTS)

            @pl.when(layer >= AHEAD)
            def _():
                for copy in fetch_turned(layer - AHEAD):
                    copy.start()

            for copy in fetch_turned(layer):
                copy.wait()
            pltpu.make_async_copy(stash_ref.at[layer], stash.at[layer], in_sems.at[layer]).wait()
            backward_layer(
                layer,
                common,
                lambda: extra[0][slot] if extra else turned_out[layer],
                lambda lanes: second[slot, :, lanes],
            )
            return carry

        lax.fori_loop(0, LAYERS, step, 0)
        sent_ref[...] = cotangent[...].astype(bf16)

        def end(layer, carry):
            pltpu.make_async_copy(wide.at[layer], stash_out.at[layer], out_sems.at[layer]).wait()
            return carry

        lax.fori_loop(0, LAYERS, end, 0)


STASH = pltpu.HBM((LAYERS, PARTS, ROWS, WIDE), bf16)
SMALL = pltpu.HBM((LAYERS, 2, ROWS, HD), f32)
SENT = jax.ShapeDtypeStruct((ROWS, D), bf16)
ANY = pl.BlockSpec(memory_space=pl.ANY)
VMEM = pl.BlockSpec(memory_space=pltpu.VMEM)
SMEM = pl.BlockSpec(memory_space=pltpu.SMEM)
STATE = [pltpu.VMEM((ROWS, D), f32), pltpu.VMEM((ROWS, D), bf16)]
PARAMS = pltpu.CompilerParams(vmem_limit_bytes=20 * 2**20)


COST = pl.CostEstimate(flops=4 * LAYERS * ROWS * D * HD, bytes_accessed=36 * 2**20, transcendentals=0)


def in_hbm(value):
    return pltpu.with_memory_space_constraint(value, pltpu.HBM)


def in_vmem(value):
    return pltpu.with_memory_space_constraint(value, pltpu.VMEM)


STREAM_IN = [pltpu.VMEM((SLOTS, D, HD), bf16), pltpu.SemaphoreType.DMA((SLOTS,))]
FORWARD = STATE + [
    pltpu.VMEM(STASH.shape, bf16),
    pltpu.VMEM(SMALL.shape, f32),
    pltpu.SemaphoreType.DMA((LAYERS + 1,)),
]


def run_turn(place, pieces, after):
    rows, columns = pieces[0].shape
    return pl.pallas_call(
        functools.partial(turn_kernel, rows > columns),
        in_specs=[SMEM] + [ANY] * 9,
        out_specs=[VMEM, ANY],
        out_shape=[
            pltpu.VMEM((LAYERS, rows, columns), bf16),
            pltpu.HBM((LAYERS, columns, rows), bf16),
        ],
        scratch_shapes=[
            pltpu.VMEM((2, columns, rows), bf16),
            pltpu.SemaphoreType.DMA((LAYERS,)),
            pltpu.SemaphoreType.DMA((2,)),
        ],
        compiler_params=pltpu.CompilerParams(vmem_limit_bytes=6 * 2**20),
        cost_estimate=COST,
        name="team_turn",
    )(place, *map(in_hbm, pieces), after)


def run_early(tick, place, x, pieces_in, pieces_out, stash, small):
    older = [] if stash is None else [stash, small]
    return pl.pallas_call(
        functools.partial(early_kernel, tick),
        in_specs=[SMEM, VMEM] + [ANY] * (16 + len(older)),
        out_specs=[VMEM, ANY, ANY],
        out_shape=[SENT, STASH, SMALL],
        input_output_aliases={18: 1, 19: 2} if older else {},
        scratch_shapes=FORWARD
        + [
            pltpu.VMEM((SLOTS, D, HD), bf16),
            pltpu.VMEM((SLOTS, HD, D), bf16),
            pltpu.SemaphoreType.DMA((SLOTS,)),
            pltpu.SemaphoreType.DMA((SLOTS,)),
        ],
        compiler_params=PARAMS,
        cost_estimate=COST,
        name="team_early",
    )(place, x, *map(in_hbm, pieces_in), *map(in_hbm, pieces_out), *map(in_hbm, older))


def run_forward(tick, place, x, held_out, weights_in, stash, small):
    resident = tick > EARLY
    weights_in = [in_vmem(weights_in)] if resident else [*map(in_hbm, weights_in)]
    count = len(weights_in)
    return pl.pallas_call(
        functools.partial(forward_kernel, tick),
        in_specs=[SMEM, VMEM, VMEM] + [VMEM if resident else ANY] * count + [ANY] * 2,
        out_specs=[VMEM, ANY, ANY],
        out_shape=[SENT, STASH, SMALL],
        input_output_aliases={3 + count: 1, 4 + count: 2},
        scratch_shapes=FORWARD + ([] if resident else STREAM_IN),
        compiler_params=pltpu.CompilerParams(vmem_limit_bytes=(6 if resident else 14) * 2**20),
        cost_estimate=COST,
        name="team_forward",
    )(place, x, in_vmem(held_out), *weights_in, in_hbm(stash), in_hbm(small))


def run_backward(tick, place, c, turned_out, turned_in, stash, small, cots):
    older = [] if cots is None else [cots]
    streams = tick == LAST
    turned_out = in_hbm(turned_out) if streams else in_vmem(turned_out)
    return pl.pallas_call(
        functools.partial(backward_kernel, tick),
        in_specs=[SMEM, VMEM, ANY if streams else VMEM] + [ANY] * (3 + len(older)),
        out_specs=[VMEM, ANY],
        out_shape=[SENT, STASH],
        input_output_aliases={6: 1} if older else {},
        scratch_shapes=STATE
        + [
            pltpu.VMEM(STASH.shape, bf16),
            pltpu.VMEM(STASH.shape, bf16),
            pltpu.VMEM(SMALL.shape, f32),
            pltpu.SemaphoreType.DMA((LAYERS + 1,)),
            pltpu.SemaphoreType.DMA((LAYERS,)),
            pltpu.VMEM((SLOTS, HD, D), bf16),
            pltpu.SemaphoreType.DMA((SLOTS,)),
        ]
        + (STREAM_IN if streams else []),
        compiler_params=pltpu.CompilerParams(vmem_limit_bytes=(24 if streams else 16) * 2**20),
        cost_estimate=COST,
        name="team_backward",
    )(place, c, turned_out, *map(in_hbm, [turned_in, stash, small, *older]))


def along_z(value, steps):
    index = [(z % 4) * 2 + z // 4 for z in range(8)]
    pairs = [(index[z], index[(z + steps) % 8]) for z in range(8)]
    return lax.ppermute(value, ("zl", "zh"), pairs)


def swap_cores(value):
    return lax.ppermute(value, "core", [(0, 1), (1, 0)])


def along_y(value, source, target):
    return lax.ppermute(value, "y", [(source, target)])


PLANE = ("zl", "core", "x", "zh")


def exchange(stash):
    flat = stash.reshape(LAYERS * PARTS, ROWS, WIDE)
    flat = lax.all_to_all(flat, PLANE, 0, 0, tiled=True)
    return flat.reshape(LAYERS * PARTS * ROWS, WIDE)


def local(inputs, gain, w_in, w_out):
    axes = ("y", "zl", "core")
    place = jnp.stack([lax.axis_index(axis) for axis in axes]).astype(jnp.int32)
    own_in, own_out = w_in[0], w_out[0]
    own_in = (own_in.astype(f32) * gain[0][:, None]).astype(bf16)
    before_in, after_out = along_z(own_in, 1), along_z(own_out, -1)
    before_out, after_in = along_z(own_out, 1), along_z(own_in, -1)
    near_in, near_out, inputs = lax.optimization_barrier((before_in, after_out, inputs))
    far_in, far_out = along_z(near_in, 1), along_z(near_out, -1)
    x = jnp.broadcast_to(inputs, (8,) + inputs.shape).reshape(64, ROWS, HD)
    x = lax.all_to_all(x, ("y", "zl", "core"), 0, 0, tiled=True)
    x = x.transpose(1, 0, 2).reshape(ROWS, D)
    (before_out, after_in, x) = lax.optimization_barrier((before_out, after_in, x))
    far_in, far_out = lax.optimization_barrier((far_in, far_out))
    pieces_in = [own_in, swap_cores(own_in), after_in, swap_cores(after_in)]
    pieces_in += [far_in, swap_cores(far_in), near_in, swap_cores(near_in)]
    pieces_out = [own_out, swap_cores(own_out), near_out, swap_cores(near_out)]
    pieces_out += [far_out, swap_cores(far_out), before_out, swap_cores(before_out)]

    stash = small = cots = None
    for tick in range(8):
        if tick > 0:
            last, x = x, along_y(x, tick - 1, tick)
        if tick < EARLY:
            x, stash, small = run_early(tick, place, x, pieces_in, pieces_out, stash, small)
            continue
        if tick == EARLY:
            held_out, turned_out = run_turn(place, pieces_out, last)
            weights_in = pieces_in
        if tick == EARLY + 1:
            weights_in, turned_in = run_turn(place, pieces_in, last)
            x, turned_in = lax.optimization_barrier((x, turned_in))
        x, stash, small = run_forward(tick, place, x, held_out, weights_in, stash, small)
    x, stash_sent = lax.optimization_barrier((x, stash))
    first = exchange(stash_sent)
    for tick in range(LAST, -1, -1):
        if tick < LAST:
            x = along_y(x, tick + 1, tick)
        x, cots = run_backward(tick, place, x, turned_out, turned_in, stash, small, cots)

    second = exchange(cots)
    part = lax.axis_index("x") * 2 + lax.axis_index("zh")
    own_gain = lax.dynamic_slice(gain, (0, part * SLICE), (1, SLICE)).reshape(SLICE, 1)
    scale = 1.0 / math.sqrt(LAYERS * PARTS * ROWS)
    rows = (((0,), (0,)), ((), ()))
    sum_in = lax.dot_general(
        first[:, :SLICE], second[:, SLICE:], rows, preferred_element_type=f32
    )
    sum_out = lax.dot_general(
        first[:, SLICE:], second[:, :SLICE], rows, preferred_element_type=f32
    )
    grad_in = (sum_in * own_gain * scale).astype(bf16)[None]
    grad_out = (sum_out * scale).astype(bf16)[None]
    return (grad_in, grad_out)


def solution(mesh):
    axes = ("y", "zl", "core", "x", "zh")
    split = Mesh(mesh.devices.reshape(8, 4, 2, 4, 2), axes)
    section, replica = ("y", "zl", "core"), ("x", "zh")
    return jax.shard_map(
        local,
        mesh=split,
        in_specs=(
            P(None, replica, section),
            P(section, None),
            P(section, None, None),
            P(section, None, None),
        ),
        out_specs=(P(section, replica, None), P(section, None, replica)),
        check_vma=False,
    )
```
